128 devices in a mesh: gx: 8 (over y, core), gy: 16 (over x, z).
Axes of the slice: x: 4, y: 4, z: 4, core: 2. Of those that a mesh axis runs over, the one named last changes fastest.
Arguments:
- density_blocks: bfloat16 [8192, 128, 128], P(('gx', 'gy')), may hold values from -0.01171875 to 0.01171875
- send_table: int32 [128, 3, 3, 8], P(('gx', 'gy')), may hold values from -1 to 63, as said below
- batch_pairs: int32 [32, 192, 4, 4], P('gx', 'gy'), may hold values from -1 to 71, as said below
- basis_values: bfloat16 [32, 192, 4, 256, 128], P('gx', 'gy'), may hold values from -6 to 6
- previous_hartree: float32 [32, 192, 256], P('gx', 'gy'), may hold values from -6 to 6
- external_potential: float32 [32, 192, 256], P('gx', 'gy'), may hold values from -6 to 6
Outputs:
- density: float32 [32, 192, 256], P('gx', 'gy')
- hartree: float32 [32, 192, 256], P('gx', 'gy')
- potential_blocks: float32 [8192, 128, 128], P(('gx', 'gy'))
The draws below stay inside these ranges and needn't reach their ends.
Inputs may be any that keep to these rules, and one draw needn't show every extreme that they name: send_table[s, i, j, c] is owner s's local index of the pair block in slot c for the brick at mesh offset (i - 1, j - 1) from s, or -1; an entry is filled exactly when some batch of that brick names the slot, is -1 toward bricks outside the mesh, and in every draw some brick has all 72 of its slots filled. `batch_pairs`: entry [n, a, b] is the received slot (k * 3 + l) * 8 + c of the density block for orbital blocks a and b of batch n, naming the owner at mesh offset (k - 1, l - 1) from the batch's brick, never one outside the mesh; -1 where the pair has no block; the share of pairs with a block varies from brick to brick.
All inputs are finite; a program needn't handle non-finite values.
Results may differ from the reference program's by a relative error of at most 0.0029.
Values may be sent and summed in bfloat16 or wider, within the bound.
No kernel may reach another device: no remote copies, remote signals or barrier semaphores. Data moves between devices by JAX's collectives and lax.ppermute only.
A program may use at most 256 MiB of HBM per device.

```python
import jax
import jax.numpy as jnp
from jax import lax

BLK = 128
KB = 4
NZ = 256
SWEEPS = 3
CAP = 8
BX = 4
BY = 12
NPB = 64
SLOTS = 72
NX = 32
NY = 192
N_GX = 8
N_GY = 16
DEVICES = 128


def shared_routes(shared_key):
    key_list = jax.random.split(shared_key, 9)
    pair_total = BX * BY * KB * KB
    device_ids = jnp.arange(DEVICES)
    brick_x = device_ids // N_GY
    brick_y = device_ids % N_GY
    live_level = jax.random.randint(key_list[0], (DEVICES, 1), 1, 5)
    coin_draws = jax.random.randint(key_list[1], (DEVICES, pair_total), 0, 4)
    live_mask = coin_draws < live_level
    step_x = jax.random.randint(key_list[2], (DEVICES, pair_total), 0, 3)
    step_y = jax.random.randint(key_list[3], (DEVICES, pair_total), 0, 3)
    slot_depth = jax.random.randint(key_list[4], (DEVICES, pair_total), 0, CAP)
    inside_x = (brick_x[:, None] + step_x - 1 >= 0) & (brick_x[:, None] + step_x - 1 < N_GX)
    inside_y = (brick_y[:, None] + step_y - 1 >= 0) & (brick_y[:, None] + step_y - 1 < N_GY)
    step_x = jnp.where(inside_x, step_x, 1)
    step_y = jnp.where(inside_y, step_y, 1)
    slot_draws = (step_x * 3 + step_y) * CAP + slot_depth
    full_x = jax.random.randint(key_list[5], (), 1, N_GX - 1)
    full_y = jax.random.randint(key_list[6], (), 1, N_GY - 1)
    full_device = full_x * N_GY + full_y
    slot_order = jax.random.permutation(key_list[7], SLOTS).astype(jnp.int32)
    padded_order = jnp.concatenate([slot_order, jnp.zeros((pair_total - SLOTS,), jnp.int32)])
    positions = jnp.arange(pair_total)[None, :]
    forced = (device_ids[:, None] == full_device) & (positions < SLOTS)
    slot_draws = jnp.where(forced, padded_order[None, :], slot_draws)
    live_mask = live_mask | forced
    slot_refs = jnp.where(live_mask, slot_draws, -1)
    used_slots = jnp.any(slot_refs[:, :, None] == jnp.arange(SLOTS)[None, None, :], axis=1)
    used_slots = used_slots.reshape(DEVICES, 3, 3, CAP)
    offset_ids = jnp.arange(3)
    target_x = brick_x[:, None] + offset_ids[None, :] - 1
    target_y = brick_y[:, None] + offset_ids[None, :] - 1
    valid = ((target_x >= 0) & (target_x < N_GX))[:, :, None] & ((target_y >= 0) & (target_y < N_GY))[:, None, :]
    target_ids = jnp.clip(target_x, 0, N_GX - 1)[:, :, None] * N_GY + jnp.clip(target_y, 0, N_GY - 1)[:, None, :]
    used_owner = used_slots[target_ids, (2 - offset_ids)[None, :, None], (2 - offset_ids)[None, None, :]]
    local_rows = jax.random.randint(key_list[8], (DEVICES, 3, 3, CAP), 0, NPB)
    top_entry = (device_ids == full_device)[:, None, None, None] & (offset_ids == 1)[None, :, None, None] & (offset_ids == 1)[None, None, :, None] & (jnp.arange(CAP) == 0)[None, None, None, :]
    local_rows = jnp.where(top_entry, NPB - 1, local_rows)
    send_rows = jnp.where(valid[..., None] & used_owner, local_rows, -1).astype(jnp.int32)
    grid_slots = slot_refs.reshape(N_GX, N_GY, BX, BY, KB, KB).transpose(0, 2, 1, 3, 4, 5)
    grid_slots = grid_slots.reshape(N_GX * BX, N_GY * BY, KB, KB).astype(jnp.int32)
    return (send_rows, grid_slots)


def draw_send_table(key, part):
    shared_key = key
    return shared_routes(shared_key)[0]


def draw_batch_pairs(key, part):
    shared_key = key
    return shared_routes(shared_key)[1]


def steps_of(stream_key, dims, pieces, low, high):
    def one(position, shards_of):
        heights = jax.random.uniform(jax.random.fold_in(jax.random.fold_in(stream_key, 6), position), (shards_of,), jnp.float32, low / len(pieces), high / len(pieces))
        return jnp.repeat(jnp.exp(heights), dims[position] // shards_of).reshape((-1,) + (1,) * (len(dims) - position - 1))

    gain = one(*pieces[0])
    for cut in pieces[1:]:
        gain = gain * one(*cut)
    return gain


def noise(own_key, shape, spread, bound, cuts=(), held_as=jnp.bfloat16):
    gain = steps_of(own_key, shape, cuts, -0.22, 0.18) if cuts else 1.0
    values = jax.random.normal(own_key, shape, jnp.float32) * spread * gain
    return jnp.minimum(jnp.maximum(values, -bound), bound).astype(held_as)


def setup_inputs(seed: int = 0) -> dict:
    splits = jax.random.split(jax.random.key(seed), 7)
    return {
        "density_blocks": noise(splits[0], (DEVICES * NPB, BLK, BLK), (BLK * BLK * KB * KB) ** -0.5, 0.01171875, ((0, 128),)),
        "send_table": draw_send_table(jax.random.fold_in(splits[6], 71), 0),
        "batch_pairs": draw_batch_pairs(jax.random.fold_in(splits[6], 71), 0),
        "basis_values": noise(splits[3], (NX, NY, KB, NZ, BLK), 1.0, 6.0, ((0, 8), (1, 16))),
        "previous_hartree": noise(splits[4], (NX, NY, NZ), 1.0, 6.0, ((0, 8), (1, 16)), jnp.float32),
        "external_potential": noise(splits[5], (NX, NY, NZ), 1.0, 6.0, ((0, 8), (1, 16)), jnp.float32),
    }


cell_volume = 0.0625


def stencil(field, charge):
    padded = jnp.pad(field, 1)
    beside = padded[2:, 1:-1, 1:-1] + padded[:-2, 1:-1, 1:-1]
    beside = beside + padded[1:-1, 2:, 1:-1] + padded[1:-1, :-2, 1:-1]
    beside = beside + padded[1:-1, 1:-1, 2:] + padded[1:-1, 1:-1, :-2]
    return (beside + charge) / 6.0


def brick_inputs(device, density_blocks, send_table, batch_pairs, basis_values):
    brick_gx = (device // N_GY).astype(jnp.int32)
    brick_gy = (device % N_GY).astype(jnp.int32)
    zero_index = jnp.zeros((), jnp.int32)
    offset_ids = jnp.arange(3, dtype=jnp.int32)
    owner_x = brick_gx + offset_ids - 1
    owner_y = brick_gy + offset_ids - 1
    valid = ((owner_x >= 0) & (owner_x < N_GX))[:, None] & ((owner_y >= 0) & (owner_y < N_GY))[None, :]
    owner_ids = jnp.clip(owner_x, 0, N_GX - 1)[:, None] * N_GY + jnp.clip(owner_y, 0, N_GY - 1)[None, :]
    rows_sent = send_table[owner_ids, (2 - offset_ids)[:, None], (2 - offset_ids)[None, :]]
    live_rows = valid[:, :, None] & (rows_sent >= 0)
    flat_rows = owner_ids[:, :, None] * NPB + rows_sent
    picked_rows = jnp.clip(flat_rows, 0, DEVICES * NPB - 1)
    received = jnp.where(live_rows[..., None, None], density_blocks[picked_rows],
                         jnp.zeros((), jnp.bfloat16)).reshape(SLOTS, BLK, BLK)
    owner_rows = jnp.where(live_rows, flat_rows, DEVICES * NPB).reshape(-1).astype(jnp.int32)
    pair_slots = lax.dynamic_slice(batch_pairs, (brick_gx * BX, brick_gy * BY, zero_index, zero_index),
                                   (BX, BY, KB, KB)).reshape(BX * BY, KB, KB)
    basis_cols = lax.dynamic_slice(basis_values, (brick_gx * BX, brick_gy * BY, zero_index, zero_index, zero_index),
                                   (BX, BY, KB, NZ, BLK)).reshape(BX * BY, KB, NZ, BLK)
    return owner_rows, received, pair_slots, basis_cols, brick_gx, brick_gy


def reference(density_blocks, send_table, batch_pairs, basis_values, previous_hartree, external_potential):
    def density_of(device):
        owner_rows, received, pair_slots, basis_cols, brick_gx, brick_gy = brick_inputs(
            device, density_blocks, send_table, batch_pairs, basis_values)
        live_mask = pair_slots >= 0
        picked = jnp.where(live_mask[..., None, None], received[jnp.clip(pair_slots, 0, SLOTS - 1)],
                           jnp.zeros((), jnp.bfloat16))
        basis_wide = basis_cols.astype(jnp.float32)
        mixed_rows = jnp.einsum('nbzv,nabuv->nazu', basis_wide, picked.astype(jnp.float32))
        return jnp.sum(basis_wide * mixed_rows, axis=(1, 3)).reshape(BX, BY, NZ)

    columns = lax.map(density_of, jnp.arange(DEVICES, dtype=jnp.int32))
    density = columns.reshape(N_GX, N_GY, BX, BY, NZ).transpose(0, 2, 1, 3, 4).reshape(N_GX * BX, N_GY * BY, NZ)
    hartree = previous_hartree
    for sweep_index in range(SWEEPS):
        hartree = stencil(hartree, density)
    total_field = hartree + external_potential

    def accumulate(potential, device):
        owner_rows, received, pair_slots, basis_cols, brick_gx, brick_gy = brick_inputs(
            device, density_blocks, send_table, batch_pairs, basis_values)
        zero_index = jnp.zeros((), jnp.int32)
        column_field = lax.dynamic_slice(total_field, (brick_gx * BX, brick_gy * BY, zero_index),
                                         (BX, BY, NZ)).reshape(BX * BY, NZ)
        basis_wide = basis_cols.astype(jnp.float32)
        weighted = (column_field[:, None, :, None] * basis_wide).astype(jnp.bfloat16)
        integrals = cell_volume * jnp.einsum('nazu,nbzv->nabuv', basis_wide, weighted.astype(jnp.float32))
        slot_target = jnp.where(pair_slots >= 0, pair_slots, SLOTS).reshape(-1).astype(jnp.int32)
        partial_value = jnp.zeros((SLOTS, BLK, BLK), jnp.float32).at[slot_target].add(
            integrals.reshape(-1, BLK, BLK), mode="drop")
        return potential.at[owner_rows].add(partial_value, mode="drop"), None

    potential, unused = lax.scan(accumulate, jnp.zeros((DEVICES * NPB, BLK, BLK), jnp.float32),
                                 jnp.arange(DEVICES, dtype=jnp.int32))
    return density, hartree, potential
```

```python
import functools

import jax
import jax.numpy as jnp
from jax import lax
from jax.experimental import pallas as pl
from jax.experimental.pallas import tpu as pltpu
from jax.sharding import PartitionSpec as P

SWEEPS = 3
CELL_VOLUME = 0.0625
VMEM_LIMIT = 56 * 1024 * 1024

KINDS = ((0, 0), (0, 1), (0, 2), (1, 1), (1, 2), (2, 1), (2, 2), (2, 0), (1, 0))


def partner(index, kind):
    if kind == 0:
        return index
    return index + 1 if index % 2 == kind - 1 else index - 1


def swap(value, kind, sizes):
    count_x, count_y = sizes
    pairs = []
    for p in range(count_x):
        for q in range(count_y):
            to_p, to_q = partner(p, kind[0]), partner(q, kind[1])
            if 0 <= to_p < count_x and 0 <= to_q < count_y:
                pairs.append((p * count_y + q, to_p * count_y + to_q))
    return lax.ppermute(value, ("gx", "gy"), pairs)


def group_ids():
    p, q = lax.axis_index("gx"), lax.axis_index("gy")

    def side(index, kind):
        if kind == 0:
            return jnp.int32(1)
        ahead = index % 2 == kind - 1
        return jnp.where(ahead, 2, 0).astype(jnp.int32)

    return jnp.stack([side(p, a) * 3 + side(q, b) for a, b in KINDS])


def call(body, name, **options):
    return pl.pallas_call(
        body,
        name=name,
        compiler_params=pltpu.CompilerParams(vmem_limit_bytes=VMEM_LIMIT),
        **options,
    )


SMEM = pl.BlockSpec(memory_space=pltpu.SMEM)
VMEM = pl.BlockSpec(memory_space=pltpu.VMEM)
ANY = pl.BlockSpec(memory_space=pl.ANY)


def gather_body(groups, table, blocks, *rest):
    outs, sems = rest[:-1], rest[-1]
    depth = table.shape[2]
    for t, out in enumerate(outs):
        k, l = groups[t] // 3, groups[t] % 3
        for c in range(depth):
            row = jnp.maximum(table[k, l, c], 0)
            pltpu.make_async_copy(blocks.at[row], out.at[c], sems.at[t]).start()
    for t, out in enumerate(outs):
        pltpu.make_async_copy(blocks.at[pl.ds(0, depth)], out, sems.at[t]).wait()


def gather(groups, table, blocks):
    depth, width = table.shape[2], blocks.shape[1]
    kinds = len(KINDS)
    return call(
        gather_body,
        "gather",
        in_specs=[SMEM, SMEM, ANY],
        out_specs=[ANY] * kinds,
        out_shape=[jax.ShapeDtypeStruct((depth, width, width), blocks.dtype)] * kinds,
        scratch_shapes=[pltpu.SemaphoreType.DMA((kinds,))],
    )(groups, table, blocks)


def transpose_body(chunk, source, out, held, turned, sems_in, sems_out):
    count, blocks, _, width = source.shape
    steps = count // chunk

    def part(c):
        return pl.ds(c * chunk, chunk)

    def coming(c):
        return pltpu.make_async_copy(source.at[part(c)], held.at[part(c)], sems_in.at[c])

    def going(c):
        return pltpu.make_async_copy(turned.at[part(c)], out.at[part(c)], sems_out.at[c])

    for c in range(steps):
        coming(c).start()
    for c in range(steps):
        coming(c).wait()
        for n in range(c * chunk, (c + 1) * chunk):
            for b in range(blocks):
                turned[n, b * width : (b + 1) * width, :] = held[n, b].T
        going(c).start()
    for c in range(steps):
        going(c).wait()


def transposed(basis, chunk=4):
    count, blocks, points, width = basis.shape
    shape = (count, blocks * width, points)
    return call(
        functools.partial(transpose_body, chunk),
        "transpose",
        in_specs=[ANY],
        out_specs=ANY,
        out_shape=jax.ShapeDtypeStruct(shape, basis.dtype),
        scratch_shapes=[
            pltpu.VMEM(basis.shape, basis.dtype),
            pltpu.VMEM(shape, basis.dtype),
            pltpu.SemaphoreType.DMA((count // chunk,)),
            pltpu.SemaphoreType.DMA((count // chunk,)),
        ],
        cost_estimate=pl.CostEstimate(flops=0, bytes_accessed=4 * basis.size, transcendentals=0),
    )(basis)


def density_body(chunk, ahead, groups, slots, basis, *rest):
    kinds = len(KINDS)
    messages, (out, held, blocks, sems, block_sems) = rest[:kinds], rest[kinds:]
    count, rows, _ = basis.shape
    depth, width, _ = messages[0].shape
    per = rows // width
    steps = count // chunk

    def coming(c):
        part = pl.ds(c * chunk, chunk)
        return pltpu.make_async_copy(basis.at[part], held.at[part], sems.at[c])

    arrivals = [
        pltpu.make_async_copy(message, blocks.at[pl.ds(groups[t] * depth, depth)], block_sems.at[t])
        for t, message in enumerate(messages)
    ]
    for copy in arrivals:
        copy.start()
    for c in range(ahead):
        coming(c).start()
    blocks[kinds * depth] = jnp.zeros((width, width), blocks.dtype)
    for copy in arrivals:
        copy.wait()

    def one(n):
        rows_of = [
            jnp.concatenate([blocks[slots[n * per * per + a * per + b]] for b in range(per)], axis=1)
            for a in range(per)
        ]
        mixed = jnp.dot(
            jnp.concatenate(rows_of, axis=0), held[n], preferred_element_type=jnp.float32
        )
        product = mixed * held[n].astype(jnp.float32)
        out[pl.ds(n, 1), :] = jnp.sum(product, axis=0, keepdims=True)

    def step(c, carry):
        @pl.when(c + ahead < steps)
        def _():
            coming(c + ahead).start()

        coming(c).wait()
        for u in range(chunk):
            one(c * chunk + u)
        return carry

    lax.fori_loop(0, steps, step, 0)


def density_of(groups, slots, basis, messages, chunk=8, ahead=2):
    count, rows, points = basis.shape
    depth, width, _ = messages[0].shape
    kinds = len(KINDS)
    return call(
        functools.partial(density_body, chunk, ahead),
        "density",
        in_specs=[SMEM, SMEM] + [ANY] * (1 + kinds),
        out_specs=VMEM,
        out_shape=jax.ShapeDtypeStruct((count, points), jnp.float32),
        scratch_shapes=[
            pltpu.VMEM(basis.shape, basis.dtype),
            pltpu.VMEM((kinds * depth + 1, width, width), basis.dtype),
            pltpu.SemaphoreType.DMA((count // chunk,)),
            pltpu.SemaphoreType.DMA((kinds,)),
        ],
    )(groups, slots, basis, *messages)


def stencil(field, charge):
    z_padded = jnp.pad(field, ((0, 0), (0, 0), (1, 1)))
    beside = z_padded[2:, 1:-1, 1:-1] + z_padded[:-2, 1:-1, 1:-1]
    beside = beside + z_padded[1:-1, 2:, 1:-1] + z_padded[1:-1, :-2, 1:-1]
    beside = beside + z_padded[1:-1, 1:-1, 2:] + z_padded[1:-1, 1:-1, :-2]
    return (beside + charge) / 6.0


def halo(field, charge, dim, axis, sizes):
    length = field.shape[dim]
    wide, thin = SWEEPS, SWEEPS - 1
    even = lax.axis_index(axis) % 2 == 0
    field_shape = list(field.shape)
    charge_shape = list(charge.shape)
    field_shape[dim], charge_shape[dim] = wide, thin
    points = field.shape[-1]

    def pack(field_start, charge_start):
        a = lax.slice_in_dim(field, field_start, field_start + wide, axis=dim)
        b = lax.slice_in_dim(charge, charge_start, charge_start + thin, axis=dim)
        return jnp.concatenate([a.reshape(-1, points), b.reshape(-1, points)], axis=0)

    low, high = pack(0, 0), pack(length - wide, length - thin)
    kinds = ((1, 0), (2, 0)) if axis == "gx" else ((0, 1), (0, 2))
    first = swap(jnp.where(even, high, low), kinds[0], sizes)
    second = swap(jnp.where(even, low, high), kinds[1], sizes)
    before, after = jnp.where(even, second, first), jnp.where(even, first, second)

    def unpack(rows):
        cut = 1
        for size in field_shape[:-1]:
            cut *= size
        return rows[:cut].reshape(field_shape), rows[cut:].reshape(charge_shape)

    (field_before, charge_before), (field_after, charge_after) = unpack(before), unpack(after)
    return (
        jnp.concatenate([field_before, field, field_after], axis=dim),
        jnp.concatenate([charge_before, charge, charge_after], axis=dim),
    )


def inside(width, brick_x, brick_y, sizes):
    p, q = lax.axis_index("gx"), lax.axis_index("gy")
    x = lax.broadcasted_iota(jnp.int32, (brick_x + 2 * width, brick_y + 2 * width, 1), 0)
    y = lax.broadcasted_iota(jnp.int32, (brick_x + 2 * width, brick_y + 2 * width, 1), 1)
    x, y = x - width + p * brick_x, y - width + q * brick_y
    return (x >= 0) & (x < sizes[0] * brick_x) & (y >= 0) & (y < sizes[1] * brick_y)


def sweeps(previous, density, sizes):
    brick_x, brick_y, _ = density.shape
    field, charge = halo(previous, density, 0, "gx", sizes)
    field, charge = halo(field, charge, 1, "gy", sizes)
    for done in range(1, SWEEPS + 1):
        width = SWEEPS - done
        field = stencil(field, charge)
        if width:
            field = jnp.where(inside(width, brick_x, brick_y, sizes), field, 0.0)
            charge = charge[1:-1, 1:-1]
    return field


def integrals_body(chunk, ahead, groups, slots, basis, potential, *rest):
    kinds = len(KINDS)
    outs, (held, sums, sems) = rest[:kinds], rest[kinds:]
    count, rows, _ = basis.shape
    depth, width, _ = outs[0].shape
    per = rows // width
    steps = count // chunk

    def coming(c):
        part = pl.ds(c * chunk, chunk)
        return pltpu.make_async_copy(basis.at[part], held.at[part], sems.at[c])

    for c in range(ahead):
        coming(c).start()
    sums[...] = jnp.zeros_like(sums)

    def one(n):
        wide = held[n].astype(jnp.float32)
        weighted = (wide * potential[pl.ds(n, 1), :]).astype(basis.dtype)
        product = lax.dot_general(
            held[n], weighted, (((1,), (1,)), ((), ())), preferred_element_type=jnp.float32
        )
        for a in range(per):
            for b in range(per):
                slot = slots[n * per * per + a * per + b]
                sums[slot] += product[a * width : (a + 1) * width, b * width : (b + 1) * width]

    def step(c, carry):
        @pl.when(c + ahead < steps)
        def _():
            coming(c + ahead).start()

        coming(c).wait()
        for u in range(chunk):
            one(c * chunk + u)
        return carry

    lax.fori_loop(0, steps, step, 0)
    for t, out in enumerate(outs):
        part = sums[pl.ds(groups[t] * depth, depth)]
        out[...] = (CELL_VOLUME * part).astype(out.dtype)


def integrals_of(groups, slots, basis, potential, depth, width, chunk=8, ahead=2):
    count, rows, _ = basis.shape
    kinds = len(KINDS)
    shape = (depth, width, width)
    return call(
        functools.partial(integrals_body, chunk, ahead),
        "integrals",
        in_specs=[SMEM, SMEM, ANY, VMEM],
        out_specs=[VMEM] * kinds,
        out_shape=[jax.ShapeDtypeStruct(shape, jnp.float32)]
        + [jax.ShapeDtypeStruct(shape, jnp.bfloat16)] * (kinds - 1),
        scratch_shapes=[
            pltpu.VMEM(basis.shape, basis.dtype),
            pltpu.VMEM((kinds * depth + 1, width, width), jnp.float32),
            pltpu.SemaphoreType.DMA((count // chunk,)),
        ],
    )(groups, slots, basis, potential)


def collect_body(groups, table, *rest):
    messages, out = rest[:-1], rest[-1]
    depth = table.shape[2]
    out[...] = jnp.zeros_like(out)
    for t, message in enumerate(messages):
        k, l = groups[t] // 3, groups[t] % 3
        for c in range(depth):
            row = table[k, l, c]

            @pl.when(row >= 0)
            def _():
                out[row] += message[c].astype(jnp.float32)


def collect(groups, table, messages, owned):
    width = messages[0].shape[1]
    return call(
        collect_body,
        "collect",
        in_specs=[SMEM, SMEM] + [VMEM] * len(messages),
        out_specs=VMEM,
        out_shape=jax.ShapeDtypeStruct((owned, width, width), jnp.float32),
    )(groups, table, *messages)


def per_device(
    sizes, density_blocks, send_table, batch_pairs, basis_values, previous_hartree, external_potential
):
    owned, width, _ = density_blocks.shape
    table = send_table[0]
    depth = table.shape[2]
    brick_x, brick_y, per, points, _ = basis_values.shape
    count = brick_x * brick_y
    groups = group_ids()
    outgoing = gather(groups, table, density_blocks)
    arrived = [outgoing[0]] + [swap(m, kind, sizes) for m, kind in zip(outgoing[1:], KINDS[1:])]
    slots = jnp.where(batch_pairs >= 0, batch_pairs, len(KINDS) * depth).reshape(-1)
    basis = transposed(basis_values.reshape(count, per, points, width))
    density = density_of(groups, slots, basis, arrived).reshape(brick_x, brick_y, points)
    hartree = sweeps(previous_hartree, density, sizes)
    field = (hartree + external_potential).reshape(count, points)
    partial = integrals_of(groups, slots, basis, field, depth, width)
    returned = [partial[0]] + [swap(m, kind, sizes) for m, kind in zip(partial[1:], KINDS[1:])]
    return density, hartree, collect(groups, table, returned, owned)


def solution(mesh):
    sizes = (mesh.shape["gx"], mesh.shape["gy"])
    in_specs = (
        P(("gx", "gy"), None, None),
        P(("gx", "gy"), None, None, None),
        P("gx", "gy", None, None),
        P("gx", "gy", None, None, None),
        P("gx", "gy", None),
        P("gx", "gy", None),
    )
    out_specs = (P("gx", "gy", None), P("gx", "gy", None), P(("gx", "gy"), None, None))
    return jax.shard_map(
        functools.partial(per_device, sizes),
        mesh=mesh,
        in_specs=in_specs,
        out_specs=out_specs,
        check_vma=False,
    )
```

```python
import functools

import jax
import jax.numpy as jnp
from jax import lax
from jax.experimental import pallas as pl
from jax.experimental.pallas import tpu as pltpu
from jax.sharding import PartitionSpec as P

SWEEPS = 3
CELL_VOLUME = 0.0625

KINDS = ((0, 0), (0, 1), (0, 2), (1, 1), (1, 2), (2, 1), (2, 2), (2, 0), (1, 0))


def partner(index, kind):
    if kind == 0:
        return index
    return index + 1 if index % 2 == kind - 1 else index - 1


def swap(value, kind, sizes):
    count_x, count_y = sizes
    pairs = []
    for p in range(count_x):
        for q in range(count_y):
            to_p, to_q = partner(p, kind[0]), partner(q, kind[1])
            if 0 <= to_p < count_x and 0 <= to_q < count_y:
                pairs.append((p * count_y + q, to_p * count_y + to_q))
    return lax.ppermute(value, ("gx", "gy"), pairs)


def group_ids():
    p, q = lax.axis_index("gx"), lax.axis_index("gy")

    def side(index, kind):
        if kind == 0:
            return 1
        return jnp.where((index & 1) == kind - 1, 2, 0)

    return [side(p, a) * 3 + side(q, b) for a, b in KINDS]


def call(body, name, megabytes, **options):
    return pl.pallas_call(
        body,
        name=name,
        compiler_params=pltpu.CompilerParams(vmem_limit_bytes=megabytes * 1024 * 1024),
        **options,
    )


SMEM = pl.BlockSpec(memory_space=pltpu.SMEM)
VMEM = pl.BlockSpec(memory_space=pltpu.VMEM)
ANY = pl.BlockSpec(memory_space=pl.ANY)


def gather_body(table, blocks, *outs):
    depth = table.shape[2]
    for group, out in zip(group_ids(), outs):
        for c in range(depth):
            out[c] = blocks[jnp.maximum(table[group, 0, c], 0)]


def gather(table, blocks):
    depth, width = table.shape[2], blocks.shape[1]
    kinds = len(KINDS)
    return call(
        gather_body,
        "gather",
        12,
        in_specs=[SMEM, VMEM],
        out_specs=[VMEM] * kinds,
        out_shape=[jax.ShapeDtypeStruct((depth, width, width), blocks.dtype)] * kinds,
    )(table, blocks)


def slot_of(slots, x, y, a, b, empty):
    slot = slots[x, a, b, y]
    return jnp.where(slot < 0, empty, slot)


def density_body(slots, basis, *rest):
    kinds = len(KINDS)
    messages, rest = rest[:kinds], rest[kinds:]
    out, turned_out, held, turned, blocks, sems_in, sems_out, block_sems = rest
    brick_x, brick_y, per, points, width = basis.shape
    depth = messages[0].shape[0]
    empty = kinds * depth

    def coming(x):
        return pltpu.make_async_copy(basis.at[x], held.at[x % 2], sems_in.at[x])

    def going(x):
        return pltpu.make_async_copy(turned.at[x % 2], turned_out.at[x], sems_out.at[x])

    arrivals = [
        pltpu.make_async_copy(message, blocks.at[pl.ds(group * depth, depth)], block_sems.at[t])
        for t, (group, message) in enumerate(zip(group_ids(), messages))
    ]
    coming(0).start()
    for copy in arrivals:
        copy.start()
    coming(1).start()
    blocks[empty] = jnp.zeros((width, width), blocks.dtype)
    for copy in arrivals:
        copy.wait()

    def one(x, y):
        side = x % 2
        for b in range(per):
            turned[side, y, b * width : (b + 1) * width, :] = held[side, y, b].T
        rows = [
            jnp.concatenate(
                [blocks[slot_of(slots, x, y, a, b, empty)] for b in range(per)], axis=1
            )
            for a in range(per)
        ]
        right = turned[side, y]
        mixed = jnp.dot(
            jnp.concatenate(rows, axis=0), right, preferred_element_type=jnp.float32
        )
        product = mixed * right.astype(jnp.float32)
        out[y, pl.ds(x, 1), :] = jnp.sum(product, axis=0, keepdims=True)

    def step(x, carry):
        coming(x).wait()

        @pl.when(x >= 2)
        def _():
            going(x - 2).wait()

        for y in range(brick_y):
            one(x, y)
        going(x).start()

        @pl.when(x + 2 < brick_x)
        def _():
            coming(x + 2).start()

        return carry

    lax.fori_loop(0, brick_x, step, 0)
    going(brick_x - 2).wait()
    going(brick_x - 1).wait()


def density_of(slots, basis, messages):
    brick_x, brick_y, per, points, width = basis.shape
    depth = messages[0].shape[0]
    kinds = len(KINDS)
    turned = (brick_x, brick_y, per * width, points)
    return call(
        density_body,
        "density",
        20,
        in_specs=[SMEM] + [ANY] * (1 + kinds),
        out_specs=[VMEM, ANY],
        out_shape=[
            jax.ShapeDtypeStruct((brick_y, brick_x, points), jnp.float32),
            jax.ShapeDtypeStruct(turned, basis.dtype),
        ],
        scratch_shapes=[
            pltpu.VMEM((2,) + basis.shape[1:], basis.dtype),
            pltpu.VMEM((2,) + turned[1:], basis.dtype),
            pltpu.VMEM((kinds * depth + 1, width, width), basis.dtype),
            pltpu.SemaphoreType.DMA((brick_x,)),
            pltpu.SemaphoreType.DMA((brick_x,)),
            pltpu.SemaphoreType.DMA((kinds,)),
        ],
    )(slots, basis, *messages)


def stencil(field, charge):
    z_padded = jnp.pad(field, ((0, 0), (0, 0), (1, 1)))
    beside = z_padded[2:, 1:-1, 1:-1] + z_padded[:-2, 1:-1, 1:-1]
    beside = beside + z_padded[1:-1, 2:, 1:-1] + z_padded[1:-1, :-2, 1:-1]
    beside = beside + z_padded[1:-1, 1:-1, 2:] + z_padded[1:-1, 1:-1, :-2]
    return (beside + charge) / 6.0


def halo(field, charge, dim, axis, sizes):
    length = field.shape[dim]
    wide, thin = SWEEPS, SWEEPS - 1
    even = lax.axis_index(axis) % 2 == 0
    field_shape = list(field.shape)
    charge_shape = list(charge.shape)
    field_shape[dim], charge_shape[dim] = wide, thin
    points = field.shape[-1]

    def pack(field_start, charge_start):
        a = lax.slice_in_dim(field, field_start, field_start + wide, axis=dim)
        b = lax.slice_in_dim(charge, charge_start, charge_start + thin, axis=dim)
        return jnp.concatenate([a.reshape(-1, points), b.reshape(-1, points)], axis=0)

    low, high = pack(0, 0), pack(length - wide, length - thin)
    kinds = ((1, 0), (2, 0)) if axis == "gx" else ((0, 1), (0, 2))
    first = swap(jnp.where(even, high, low), kinds[0], sizes)
    second = swap(jnp.where(even, low, high), kinds[1], sizes)
    before, after = jnp.where(even, second, first), jnp.where(even, first, second)

    def unpack(rows):
        cut = 1
        for size in field_shape[:-1]:
            cut *= size
        return rows[:cut].reshape(field_shape), rows[cut:].reshape(charge_shape)

    (field_before, charge_before), (field_after, charge_after) = unpack(before), unpack(after)
    return (
        jnp.concatenate([field_before, field, field_after], axis=dim),
        jnp.concatenate([charge_before, charge, charge_after], axis=dim),
    )


def inside(width, brick_x, brick_y, sizes):
    p, q = lax.axis_index("gx"), lax.axis_index("gy")
    shape = (brick_y + 2 * width, brick_x + 2 * width, 1)
    y = lax.broadcasted_iota(jnp.int32, shape, 0) - width + q * brick_y
    x = lax.broadcasted_iota(jnp.int32, shape, 1) - width + p * brick_x
    return (x >= 0) & (x < sizes[0] * brick_x) & (y >= 0) & (y < sizes[1] * brick_y)


def sweeps(previous, density, sizes):
    brick_y, brick_x, _ = density.shape
    field, charge = halo(previous, density, 1, "gx", sizes)
    field, charge = halo(field, charge, 0, "gy", sizes)
    for done in range(1, SWEEPS + 1):
        width = SWEEPS - done
        field = stencil(field, charge)
        if width:
            field = jnp.where(inside(width, brick_x, brick_y, sizes), field, 0.0)
            charge = charge[1:-1, 1:-1]
    return field


def integrals_body(unroll, slots, basis, potential, *rest):
    kinds = len(KINDS)
    outs, (held, sums, sems) = rest[:kinds], rest[kinds:]
    brick_x, brick_y, rows, _ = basis.shape
    depth, width, _ = outs[0].shape
    per = rows // width
    empty = kinds * depth

    def coming(x):
        return pltpu.make_async_copy(basis.at[x], held.at[x % 2], sems.at[x])

    coming(0).start()
    coming(1).start()
    sums[...] = jnp.zeros_like(sums)

    def one(x, y):
        left = held[x % 2, y]
        weighted = (left.astype(jnp.float32) * potential[y, pl.ds(x, 1), :]).astype(basis.dtype)
        product = lax.dot_general(
            left, weighted, (((1,), (1,)), ((), ())), preferred_element_type=jnp.float32
        )
        for a in range(per):
            for b in range(per):
                slot = slot_of(slots, x, y, a, b, empty)
                sums[slot] += product[a * width : (a + 1) * width, b * width : (b + 1) * width]

    def step(x, carry):
        coming(x).wait()

        def some(j, carry):
            for u in range(unroll):
                one(x, j * unroll + u)
            return carry

        lax.fori_loop(0, brick_y // unroll, some, 0)

        @pl.when(x + 2 < brick_x)
        def _():
            coming(x + 2).start()

        return carry

    lax.fori_loop(0, brick_x, step, 0)
    for group, out in zip(group_ids(), outs):
        part = sums[pl.ds(group * depth, depth)]
        out[...] = (CELL_VOLUME * part).astype(out.dtype)


def integrals_of(slots, basis, potential, depth, width, unroll=6):
    brick_x = basis.shape[0]
    kinds = len(KINDS)
    shape = (depth, width, width)
    return call(
        functools.partial(integrals_body, unroll),
        "integrals",
        20,
        in_specs=[SMEM, ANY, VMEM],
        out_specs=[VMEM] * kinds,
        out_shape=[jax.ShapeDtypeStruct(shape, jnp.float32)]
        + [jax.ShapeDtypeStruct(shape, jnp.bfloat16)] * (kinds - 1),
        scratch_shapes=[
            pltpu.VMEM((2,) + basis.shape[1:], basis.dtype),
            pltpu.VMEM((kinds * depth + 1, width, width), jnp.float32),
            pltpu.SemaphoreType.DMA((brick_x,)),
        ],
    )(slots, basis, potential)


def collect_body(table, *rest):
    messages, out = rest[:-1], rest[-1]
    depth = table.shape[2]
    out[...] = jnp.zeros_like(out)
    for group, message in zip(group_ids(), messages):
        for c in range(depth):
            row = table[group, 0, c]

            @pl.when(row >= 0)
            def _():
                out[row] += message[c].astype(jnp.float32)


def collect(table, messages, owned):
    width = messages[0].shape[1]
    return call(
        collect_body,
        "collect",
        12,
        in_specs=[SMEM] + [VMEM] * len(messages),
        out_specs=VMEM,
        out_shape=jax.ShapeDtypeStruct((owned, width, width), jnp.float32),
    )(table, *messages)


def per_device(
    sizes, density_blocks, send_table, batch_pairs, basis_values, previous_hartree, external_potential
):
    owned, width, _ = density_blocks.shape
    depth = send_table.shape[3]
    table = send_table.reshape(9, 1, depth)
    slots = batch_pairs.transpose(0, 2, 3, 1)
    outgoing = gather(table, density_blocks)
    arrived = [outgoing[0]] + [swap(m, kind, sizes) for m, kind in zip(outgoing[1:], KINDS[1:])]
    density, basis = density_of(slots, basis_values, arrived)
    hartree = sweeps(previous_hartree.transpose(1, 0, 2), density, sizes)
    field = hartree + external_potential.transpose(1, 0, 2)
    partial = integrals_of(slots, basis, field, depth, width)
    returned = [partial[0]] + [swap(m, kind, sizes) for m, kind in zip(partial[1:], KINDS[1:])]
    potential = collect(table, returned, owned)
    return density.transpose(1, 0, 2), hartree.transpose(1, 0, 2), potential


def solution(mesh):
    sizes = (mesh.shape["gx"], mesh.shape["gy"])
    in_specs = (
        P(("gx", "gy"), None, None),
        P(("gx", "gy"), None, None, None),
        P("gx", "gy", None, None),
        P("gx", "gy", None, None, None),
        P("gx", "gy", None),
        P("gx", "gy", None),
    )
    out_specs = (P("gx", "gy", None), P("gx", "gy", None), P(("gx", "gy"), None, None))
    return jax.shard_map(
        functools.partial(per_device, sizes),
        mesh=mesh,
        in_specs=in_specs,
        out_specs=out_specs,
        check_vma=False,
    )
```

```python
import functools

import jax
import jax.numpy as jnp
from jax import lax
from jax.experimental import pallas as pl
from jax.experimental.pallas import tpu as pltpu
from jax.sharding import PartitionSpec as P

SWEEPS = 3
CELL_VOLUME = 0.0625

KINDS = ((0, 0), (0, 1), (0, 2), (1, 1), (1, 2), (2, 1), (2, 2), (2, 0), (1, 0))
SENT = (((0, 0),), ((1, 0), (1, 1), (1, 2)), ((2, 0), (2, 1), (2, 2)), ((0, 1),), ((0, 2),))
ARRIVED = (((0, 0),), ((1, 0),), ((2, 0),), ((0, 1), (1, 1)), ((0, 2), (1, 2)), ((2, 1),), ((2, 2),))


def partner(index, kind):
    if kind == 0:
        return index
    return index + 1 if index % 2 == kind - 1 else index - 1


def swap(value, kind, sizes):
    count_x, count_y = sizes
    pairs = []
    for p in range(count_x):
        for q in range(count_y):
            to_p, to_q = partner(p, kind[0]), partner(q, kind[1])
            if 0 <= to_p < count_x and 0 <= to_q < count_y:
                pairs.append((p * count_y + q, to_p * count_y + to_q))
    return lax.ppermute(value, ("gx", "gy"), pairs)


def group_ids():
    p, q = lax.axis_index("gx"), lax.axis_index("gy")

    def side(index, kind):
        if kind == 0:
            return 1
        return jnp.where((index & 1) == kind - 1, 2, 0)

    return [side(p, a) * 3 + side(q, b) for a, b in KINDS]


def call(body, name, megabytes, **options):
    return pl.pallas_call(
        body,
        name=name,
        compiler_params=pltpu.CompilerParams(vmem_limit_bytes=megabytes * 1024 * 1024),
        **options,
    )


SMEM = pl.BlockSpec(memory_space=pltpu.SMEM)
VMEM = pl.BlockSpec(memory_space=pltpu.VMEM)
ANY = pl.BlockSpec(memory_space=pl.ANY)


def gather_body(table, blocks, *outs):
    depth = table.shape[2]
    groups = dict(zip(KINDS, group_ids()))
    for out, kinds in zip(outs, SENT):
        for part, kind in enumerate(kinds):
            for c in range(depth):
                row = jnp.maximum(table[groups[kind], 0, c], 0)
                out[part * depth + c] = blocks[row]


def gather(table, blocks):
    depth, width = table.shape[2], blocks.shape[1]
    return call(
        gather_body,
        "gather",
        12,
        in_specs=[SMEM, VMEM],
        out_specs=[VMEM] * len(SENT),
        out_shape=[
            jax.ShapeDtypeStruct((len(kinds) * depth, width, width), blocks.dtype)
            for kinds in SENT
        ],
    )(table, blocks)


def spread(outgoing, depth, sizes):
    own, to_first, to_second, along_first, along_second = outgoing
    first = swap(to_first, (1, 0), sizes)
    second = swap(to_second, (2, 0), sizes)
    one = swap(jnp.concatenate([along_first, first[depth : 2 * depth]]), (0, 1), sizes)
    two = swap(jnp.concatenate([along_second, first[2 * depth :]]), (0, 2), sizes)
    three = swap(second[depth : 2 * depth], (0, 1), sizes)
    four = swap(second[2 * depth :], (0, 2), sizes)
    return [own, first, second, one, two, three, four]


def transpose_body(basis, after, turned, held, sems):
    brick_x, brick_y, per, _, width = basis.shape
    half = brick_y // 2
    parts = [(x, j) for x in range(brick_x) for j in range(2)]

    def coming(i):
        x, j = parts[i]
        here = pl.ds(j * half, half)
        return pltpu.make_async_copy(basis.at[x, here], held.at[x, here], sems.at[i])

    for i in range(len(parts)):
        coming(i).start()
    for i, (x, j) in enumerate(parts):
        coming(i).wait()
        for y in range(j * half, (j + 1) * half):
            for b in range(per):
                turned[x, y, b * width : (b + 1) * width, :] = held[x, y, b].T


def transposed(basis, after):
    brick_x, brick_y, per, points, width = basis.shape
    return call(
        transpose_body,
        "transpose",
        32,
        in_specs=[ANY, ANY],
        out_specs=VMEM,
        out_shape=pltpu.VMEM((brick_x, brick_y, per * width, points), basis.dtype),
        scratch_shapes=[
            pltpu.VMEM(basis.shape, basis.dtype),
            pltpu.SemaphoreType.DMA((2 * brick_x,)),
        ],
        cost_estimate=pl.CostEstimate(flops=0, bytes_accessed=4 * basis.size, transcendentals=0),
    )(basis, after)


def slot_of(slots, x, y, a, b, empty):
    slot = slots[x, a, b, y]
    return jnp.where(slot < 0, empty, slot)


def density_body(unroll, depth, slots, turned, previous, *rest):
    arrived, (density, to_first, to_second, kept, blocks, sems) = rest[: len(ARRIVED)], rest[len(ARRIVED) :]
    brick_x, brick_y, rows, points = turned.shape
    width = arrived[0].shape[1]
    per = rows // width
    empty = len(KINDS) * depth
    groups = dict(zip(KINDS, group_ids()))
    copies = []
    for message, kinds in zip(arrived, ARRIVED):
        for part, kind in enumerate(kinds):
            copies.append(
                pltpu.make_async_copy(
                    message.at[pl.ds(part * depth, depth)],
                    blocks.at[pl.ds(groups[kind] * depth, depth)],
                    sems.at[len(copies)],
                )
            )
    for copy in copies:
        copy.start()
    blocks[empty] = jnp.zeros((width, width), blocks.dtype)
    for copy in copies:
        copy.wait()

    def one(x, y):
        lefts = [
            jnp.concatenate(
                [blocks[slot_of(slots, x, y, a, b, empty)] for b in range(per)], axis=1
            )
            for a in range(per)
        ]
        right = turned[x, y]
        mixed = jnp.dot(jnp.concatenate(lefts, axis=0), right, preferred_element_type=jnp.float32)
        product = mixed * right.astype(jnp.float32)
        kept[y, pl.ds(x, 1), :] = jnp.sum(product, axis=0, keepdims=True)

    def step(x, carry):
        def some(j, carry):
            for u in range(unroll):
                one(x, j * unroll + u)
            return carry

        return lax.fori_loop(0, brick_y // unroll, some, carry)

    lax.fori_loop(0, brick_x, step, 0)
    density[...] = kept[...]
    even = (lax.axis_index("gx") & 1) == 0
    wide, thin = SWEEPS, SWEEPS - 1
    low = [previous[:, :wide, :], kept[:, :thin, :]]
    high = [previous[:, brick_x - wide :, :], kept[:, brick_x - thin :, :]]
    for out, where_even, where_odd in ((to_first, high, low), (to_second, low, high)):
        out[...] = jnp.zeros_like(out)
        out[:, :wide, :] = jnp.where(even, where_even[0], where_odd[0])
        out[:, wide : wide + thin, :] = jnp.where(even, where_even[1], where_odd[1])


def density_of(slots, turned, previous, arrived, depth, unroll=12):
    brick_x, brick_y, rows, points = turned.shape
    width = arrived[0].shape[1]
    kinds = len(KINDS)
    shape = (brick_y, brick_x, points)
    message = jax.ShapeDtypeStruct((brick_y, 8, points), jnp.float32)
    return call(
        functools.partial(density_body, unroll, depth),
        "density",
        12,
        in_specs=[SMEM, VMEM, VMEM] + [ANY] * len(arrived),
        out_specs=[VMEM] * 4,
        out_shape=[jax.ShapeDtypeStruct(shape, jnp.float32), message, message]
        + [jax.ShapeDtypeStruct(shape, jnp.float32)],
        scratch_shapes=[
            pltpu.VMEM((kinds * depth + 1, width, width), turned.dtype),
            pltpu.SemaphoreType.DMA((kinds,)),
        ],
    )(slots, turned, previous, *arrived)


def sides(axis, first, second):
    even = (lax.axis_index(axis) & 1) == 0
    return jnp.where(even, second, first), jnp.where(even, first, second)


def widen_body(previous, density, first, second, field, charge, to_first, to_second):
    wide, thin = SWEEPS, SWEEPS - 1
    brick_y, brick_x, points = density.shape
    before, after = sides("gx", first[...], second[...])
    field[...] = jnp.zeros_like(field)
    field[:, :wide, :] = before[:, :wide, :]
    field[:, wide : wide + brick_x, :] = previous[...]
    field[:, wide + brick_x : 2 * wide + brick_x, :] = after[:, :wide, :]
    charge[:, :thin, :] = before[:, wide : wide + thin, :]
    charge[:, thin : thin + brick_x, :] = density[...]
    charge[:, thin + brick_x :, :] = after[:, wide : wide + thin, :]
    width = brick_x + 2 * thin
    even = (lax.axis_index("gy") & 1) == 0
    low = [field[:wide, 1 : 1 + width, :], charge[:thin]]
    high = [field[brick_y - wide :, 1 : 1 + width, :], charge[brick_y - thin :]]
    for out, where_even, where_odd in ((to_first, high, low), (to_second, low, high)):
        out[:wide] = jnp.where(even, where_even[0], where_odd[0])
        out[wide:] = jnp.where(even, where_even[1], where_odd[1])


def widen(previous, density, first, second):
    brick_y, brick_x, points = density.shape
    wide, thin = SWEEPS, SWEEPS - 1
    width = brick_x + 2 * thin
    shapes = [(brick_y, 16, points), (brick_y, width, points)] + [(wide + thin, width, points)] * 2
    return call(
        widen_body,
        "widen",
        4,
        in_specs=[VMEM] * 4,
        out_specs=[VMEM] * 4,
        out_shape=[jax.ShapeDtypeStruct(shape, jnp.float32) for shape in shapes],
    )(previous, density, first, second)


def sweeps_in(field_x, charge_x, first, second, sizes, field, charge, steps):
    wide, thin = SWEEPS, SWEEPS - 1
    brick_y, width, points = charge_x.shape
    brick_x = width - 2 * thin
    before, after = sides("gy", first[...], second[...])
    field[...] = jnp.zeros_like(field)
    field[:wide, 1 : 1 + width, :] = before[:wide]
    field[wide : wide + brick_y] = field_x[...]
    field[wide + brick_y :, 1 : 1 + width, :] = after[:wide]
    charge[:thin] = before[wide:]
    charge[thin : thin + brick_y] = charge_x[...]
    charge[thin + brick_y :] = after[wide:]
    p, q = lax.axis_index("gx"), lax.axis_index("gy")
    source = field
    for done in range(1, SWEEPS + 1):
        margin = SWEEPS - done
        rows, columns = brick_y + 2 * margin, brick_x + 2 * margin
        here = source[1 : 1 + rows, 1 : 1 + columns, :]
        z = lax.broadcasted_iota(jnp.int32, here.shape, 2)
        total = source[:rows, 1 : 1 + columns, :] + source[2 : 2 + rows, 1 : 1 + columns, :]
        total += source[1 : 1 + rows, :columns, :] + source[1 : 1 + rows, 2 : 2 + columns, :]
        total += jnp.where(z == 0, 0.0, pltpu.roll(here, 1, 2))
        total += jnp.where(z == points - 1, 0.0, pltpu.roll(here, points - 1, 2))
        skip = thin - margin
        value = (total + charge[skip : skip + rows, skip : skip + columns, :]) / 6.0
        if margin == 0:
            return value
        y = lax.broadcasted_iota(jnp.int32, value.shape, 0) - margin + q * brick_y
        x = lax.broadcasted_iota(jnp.int32, value.shape, 1) - margin + p * brick_x
        known = (x >= 0) & (x < sizes[0] * brick_x) & (y >= 0) & (y < sizes[1] * brick_y)
        source = steps[done - 1]
        source[:, :columns, :] = jnp.where(known, value, 0.0)


def integrals_body(unroll, depth, sizes, slots, turned, external, *rest):
    kinds = len(KINDS)
    wide, rest = rest[:4], rest[4:]
    hartree, outs = rest[0], rest[1 : 1 + kinds]
    potential, sums, field, charge, *steps = rest[1 + kinds :]
    brick_x, brick_y, rows, _ = turned.shape
    width = outs[0].shape[1]
    per = rows // width
    empty = kinds * depth
    sums[...] = jnp.zeros_like(sums)
    swept = sweeps_in(*wide, sizes, field, charge, steps)
    hartree[...] = swept
    potential[...] = swept + external[...]

    def one(x, y):
        left = turned[x, y]
        weighted = (left.astype(jnp.float32) * potential[y, pl.ds(x, 1), :]).astype(turned.dtype)
        product = lax.dot_general(
            left, weighted, (((1,), (1,)), ((), ())), preferred_element_type=jnp.float32
        )
        for a in range(per):
            for b in range(per):
                slot = slot_of(slots, x, y, a, b, empty)
                sums[slot] += product[a * width : (a + 1) * width, b * width : (b + 1) * width]

    def step(x, carry):
        def some(j, carry):
            for u in range(unroll):
                one(x, j * unroll + u)
            return carry

        return lax.fori_loop(0, brick_y // unroll, some, carry)

    lax.fori_loop(0, brick_x, step, 0)
    for group, out in zip(group_ids(), outs):
        part = sums[pl.ds(group * depth, depth)]
        out[...] = (CELL_VOLUME * part).astype(out.dtype)


def integrals_of(slots, turned, external, wide, depth, width, sizes, unroll=6):
    brick_y, brick_x, points = external.shape
    kinds = len(KINDS)
    shape = (depth, width, width)
    return call(
        functools.partial(integrals_body, unroll, depth, sizes),
        "integrals",
        16,
        in_specs=[SMEM] + [VMEM] * 6,
        out_specs=[VMEM] * (1 + kinds),
        out_shape=[jax.ShapeDtypeStruct(external.shape, jnp.float32)]
        + [jax.ShapeDtypeStruct(shape, jnp.float32)]
        + [jax.ShapeDtypeStruct(shape, jnp.bfloat16)] * (kinds - 1),
        scratch_shapes=[
            pltpu.VMEM(external.shape, jnp.float32),
            pltpu.VMEM((kinds * depth + 1, width, width), jnp.float32),
            pltpu.VMEM((brick_y + 2 * SWEEPS, 16, points), jnp.float32),
            pltpu.VMEM((brick_y + 2 * SWEEPS - 2, brick_x + 2 * SWEEPS - 2, points), jnp.float32),
        ]
        + [
            pltpu.VMEM((brick_y + 2 * margin, 8, points), jnp.float32)
            for margin in range(SWEEPS - 1, 0, -1)
        ],
    )(slots, turned, external, *wide)


def collect_body(table, *rest):
    messages, out = rest[:-1], rest[-1]
    depth = table.shape[2]
    out[...] = jnp.zeros_like(out)
    for group, message in zip(group_ids(), messages):
        for c in range(depth):
            row = table[group, 0, c]

            @pl.when(row >= 0)
            def _():
                out[row] += message[c].astype(jnp.float32)


def collect(table, messages, owned):
    width = messages[0].shape[1]
    return call(
        collect_body,
        "collect",
        12,
        in_specs=[SMEM] + [VMEM] * len(messages),
        out_specs=VMEM,
        out_shape=jax.ShapeDtypeStruct((owned, width, width), jnp.float32),
    )(table, *messages)


def per_device(
    sizes, density_blocks, send_table, batch_pairs, basis_values, previous_hartree, external_potential
):
    owned, width, _ = density_blocks.shape
    depth = send_table.shape[3]
    table = send_table.reshape(9, 1, depth)
    slots = batch_pairs.transpose(0, 2, 3, 1)
    previous = previous_hartree.transpose(1, 0, 2)
    external = external_potential.transpose(1, 0, 2)
    arrived = spread(gather(table, density_blocks), depth, sizes)
    turned = transposed(basis_values, arrived[2])
    density, to_first, to_second, kept = density_of(slots, turned, previous, arrived, depth)
    first, second = swap(to_first, (1, 0), sizes), swap(to_second, (2, 0), sizes)
    field, charge, to_first, to_second = widen(previous, kept, first, second)
    first, second = swap(to_first, (0, 1), sizes), swap(to_second, (0, 2), sizes)
    wide = (field, charge, first, second)
    hartree, *partial = integrals_of(slots, turned, external, wide, depth, width, sizes)
    returned = [partial[0]] + [swap(m, kind, sizes) for m, kind in zip(partial[1:], KINDS[1:])]
    potential = collect(table, returned, owned)
    return density.transpose(1, 0, 2), hartree.transpose(1, 0, 2), potential


def solution(mesh):
    sizes = (mesh.shape["gx"], mesh.shape["gy"])
    in_specs = (
        P(("gx", "gy"), None, None),
        P(("gx", "gy"), None, None, None),
        P("gx", "gy", None, None),
        P("gx", "gy", None, None, None),
        P("gx", "gy", None),
        P("gx", "gy", None),
    )
    out_specs = (P("gx", "gy", None), P("gx", "gy", None), P(("gx", "gy"), None, None))
    return jax.shard_map(
        functools.partial(per_device, sizes),
        mesh=mesh,
        in_specs=in_specs,
        out_specs=out_specs,
        check_vma=False,
    )
```

```python
import functools

import jax
import jax.numpy as jnp
from jax import lax
from jax.experimental import pallas as pl
from jax.experimental.pallas import tpu as pltpu
from jax.sharding import PartitionSpec as P

SWEEPS = 3
CELL_VOLUME = 0.0625

KINDS = ((0, 0), (0, 1), (0, 2), (1, 1), (1, 2), (2, 1), (2, 2), (2, 0), (1, 0))
SENT = (((0, 0),), ((1, 0), (1, 1), (1, 2)), ((2, 0), (2, 1), (2, 2)), ((0, 1),), ((0, 2),))
ARRIVED = (((0, 0),), ((1, 0),), ((2, 0),), ((0, 1), (1, 1)), ((0, 2), (1, 2)), ((2, 1),), ((2, 2),))


def partner(index, kind):
    if kind == 0:
        return index
    return index + 1 if index % 2 == kind - 1 else index - 1


def swap(value, kind, sizes):
    count_x, count_y = sizes
    pairs = []
    for p in range(count_x):
        for q in range(count_y):
            to_p, to_q = partner(p, kind[0]), partner(q, kind[1])
            if 0 <= to_p < count_x and 0 <= to_q < count_y:
                pairs.append((p * count_y + q, to_p * count_y + to_q))
    return lax.ppermute(value, ("gx", "gy"), pairs)


def group_ids():
    p, q = lax.axis_index("gx"), lax.axis_index("gy")

    def side(index, kind):
        if kind == 0:
            return 1
        return jnp.where((index & 1) == kind - 1, 2, 0)

    return [side(p, a) * 3 + side(q, b) for a, b in KINDS]


def call(body, name, megabytes, **options):
    return pl.pallas_call(
        body,
        name=name,
        compiler_params=pltpu.CompilerParams(vmem_limit_bytes=megabytes * 1024 * 1024),
        **options,
    )


SMEM = pl.BlockSpec(memory_space=pltpu.SMEM)
VMEM = pl.BlockSpec(memory_space=pltpu.VMEM)
ANY = pl.BlockSpec(memory_space=pl.ANY)
HBM = pl.BlockSpec(memory_space=pltpu.HBM)


def gather_body(table_far, blocks_far, *rest):
    outs, (table, blocks, sems) = rest[: len(SENT)], rest[len(SENT) :]
    depth = table.shape[2]
    copies = [
        pltpu.make_async_copy(table_far, table, sems.at[0]),
        pltpu.make_async_copy(blocks_far, blocks, sems.at[1]),
    ]
    for copy in copies:
        copy.start()
    for copy in copies:
        copy.wait()
    groups = dict(zip(KINDS, group_ids()))
    for out, kinds in zip(outs, SENT):
        for part, kind in enumerate(kinds):
            for c in range(depth):
                row = jnp.maximum(table[groups[kind], 0, c], 0)
                out[part * depth + c] = blocks[row]


def gather(table, blocks):
    depth, width = table.shape[2], blocks.shape[1]
    return call(
        gather_body,
        "gather",
        12,
        in_specs=[HBM, HBM],
        out_specs=[VMEM] * len(SENT),
        out_shape=[
            jax.ShapeDtypeStruct((len(kinds) * depth, width, width), blocks.dtype)
            for kinds in SENT
        ],
        scratch_shapes=[
            pltpu.SMEM(table.shape, table.dtype),
            pltpu.VMEM(blocks.shape, blocks.dtype),
            pltpu.SemaphoreType.DMA((2,)),
        ],
    )(table, blocks)


def spread(outgoing, depth, sizes):
    own, to_first, to_second, along_first, along_second = outgoing
    first = swap(to_first, (1, 0), sizes)
    second = swap(to_second, (2, 0), sizes)
    one = swap(jnp.concatenate([along_first, first[depth : 2 * depth]]), (0, 1), sizes)
    two = swap(jnp.concatenate([along_second, first[2 * depth :]]), (0, 2), sizes)
    three = swap(second[depth : 2 * depth], (0, 1), sizes)
    four = swap(second[2 * depth :], (0, 2), sizes)
    return [own, first, second, one, two, three, four]


def transpose_body(basis, after, turned, held, sems):
    brick_x, brick_y, per, _, width = basis.shape
    half = brick_y // 2
    parts = [(x, j) for x in range(brick_x) for j in range(2)]

    def coming(i):
        x, j = parts[i]
        here = pl.ds(j * half, half)
        return pltpu.make_async_copy(basis.at[x, here], held.at[x, here], sems.at[i])

    for i in range(len(parts)):
        coming(i).start()
    for i, (x, j) in enumerate(parts):
        coming(i).wait()
        for y in range(j * half, (j + 1) * half):
            for b in range(per):
                turned[x, y, b * width : (b + 1) * width, :] = held[x, y, b].T


def transposed(basis, after):
    brick_x, brick_y, per, points, width = basis.shape
    return call(
        transpose_body,
        "transpose",
        32,
        in_specs=[ANY, ANY],
        out_specs=VMEM,
        out_shape=pltpu.VMEM((brick_x, brick_y, per * width, points), basis.dtype),
        scratch_shapes=[
            pltpu.VMEM(basis.shape, basis.dtype),
            pltpu.SemaphoreType.DMA((2 * brick_x,)),
        ],
        cost_estimate=pl.CostEstimate(flops=0, bytes_accessed=4 * basis.size, transcendentals=0),
    )(basis, after)


def slot_of(slots, x, y, a, b, empty):
    slot = slots[x, a, b, y]
    return jnp.where(slot < 0, empty, slot)


def message_of(out, previous, density, low):
    brick_y, brick_x, _ = previous.shape
    thin = SWEEPS - 1
    out[:brick_y] = previous[...]
    per = brick_x // thin
    for y in range(brick_y):
        layers = jnp.where(low, density[y, :thin, :], density[y, brick_x - thin :, :])
        out[brick_y + y // per, (y % per) * thin : (y % per + 1) * thin, :] = layers


def density_body(depth, slots, turned, previous, *rest):
    arrived, (to_first, to_second, kept, blocks) = rest[: len(ARRIVED)], rest[len(ARRIVED) :]
    brick_x, brick_y, rows, _ = turned.shape
    width = blocks.shape[1]
    per = rows // width
    empty = len(KINDS) * depth
    groups = dict(zip(KINDS, group_ids()))
    for message, kinds in zip(arrived, ARRIVED):
        for part, kind in enumerate(kinds):
            blocks[pl.ds(groups[kind] * depth, depth)] = message[part * depth : (part + 1) * depth]
    blocks[empty] = jnp.zeros((width, width), blocks.dtype)

    def step(x, carry):
        for y in range(brick_y):
            lefts = [
                jnp.concatenate(
                    [blocks[slot_of(slots, x, y, a, b, empty)] for b in range(per)], axis=1
                )
                for a in range(per)
            ]
            right = turned[x, y]
            mixed = jnp.dot(
                jnp.concatenate(lefts, axis=0), right, preferred_element_type=jnp.float32
            )
            product = mixed * right.astype(jnp.float32)
            kept[y, pl.ds(x, 1), :] = jnp.sum(product, axis=0, keepdims=True)
        return carry

    lax.fori_loop(0, brick_x, step, 0)
    odd = (lax.axis_index("gx") & 1) == 1
    message_of(to_first, previous, kept, odd)
    message_of(to_second, previous, kept, jnp.logical_not(odd))


def density_of(slots, turned, previous, arrived, depth):
    brick_x, brick_y, rows, points = turned.shape
    width = arrived[0].shape[1]
    thin = SWEEPS - 1
    shape = (brick_y, brick_x, points)
    message = jax.ShapeDtypeStruct((brick_y + brick_y * thin // brick_x, brick_x, points), jnp.float32)
    return call(
        functools.partial(density_body, depth),
        "density",
        12,
        in_specs=[SMEM] + [VMEM] * (2 + len(arrived)),
        out_specs=[VMEM] * 3,
        out_shape=[message, message, pltpu.VMEM(shape, jnp.float32)],
        scratch_shapes=[pltpu.VMEM((len(KINDS) * depth + 1, width, width), turned.dtype)],
    )(slots, turned, previous, *arrived)


def copied_body(kept, density, sums):
    density[...] = kept[...]
    sums[...] = jnp.zeros_like(sums)


def copied(kept, shape):
    return call(
        copied_body,
        "copied",
        4,
        in_specs=[VMEM],
        out_specs=[VMEM] * 2,
        out_shape=[jax.ShapeDtypeStruct(kept.shape, kept.dtype), pltpu.VMEM(shape, jnp.float32)],
    )(kept)


def cost(flops):
    return pl.CostEstimate(flops=flops, bytes_accessed=0, transcendentals=0)


def sides(axis, first, second):
    even = (lax.axis_index(axis) & 1) == 0
    return jnp.where(even, second, first), jnp.where(even, first, second)


def widen_body(previous, density, first, second, field, charge, to_first, to_second):
    wide, thin = SWEEPS, SWEEPS - 1
    brick_y, brick_x, points = density.shape
    per = brick_x // thin
    before, after = sides("gx", first[...], second[...])
    field[...] = jnp.zeros_like(field)
    field[:, :wide, :] = before[:brick_y, brick_x - wide :, :]
    field[:, wide : wide + brick_x, :] = previous[...]
    field[:, wide + brick_x : 2 * wide + brick_x, :] = after[:brick_y, :wide, :]
    charge[:, thin : thin + brick_x, :] = density[...]
    for y in range(brick_y):
        row, start = brick_y + y // per, (y % per) * thin
        charge[y, :thin, :] = before[row, start : start + thin, :]
        charge[y, thin + brick_x :, :] = after[row, start : start + thin, :]
    width = brick_x + 2 * thin
    even = (lax.axis_index("gy") & 1) == 0
    low = [field[:wide, 1 : 1 + width, :], charge[:thin]]
    high = [field[brick_y - wide :, 1 : 1 + width, :], charge[brick_y - thin :]]
    for out, where_even, where_odd in ((to_first, high, low), (to_second, low, high)):
        out[:wide] = jnp.where(even, where_even[0], where_odd[0])
        out[wide:] = jnp.where(even, where_even[1], where_odd[1])


def widen(previous, density, first, second):
    brick_y, brick_x, points = density.shape
    wide, thin = SWEEPS, SWEEPS - 1
    width = brick_x + 2 * thin
    shapes = [(brick_y, 16, points), (brick_y, width, points)] + [(wide + thin, width, points)] * 2
    return call(
        widen_body,
        "widen",
        4,
        in_specs=[VMEM] * 4,
        out_specs=[VMEM] * 4,
        out_shape=[jax.ShapeDtypeStruct(shape, jnp.float32) for shape in shapes],
    )(previous, density, first, second)


def sweeps_in(field, field_y, charge, charge_y, first, last, brick_y, sizes, steps):
    points = field.shape[2]
    brick_x = charge.shape[1] - 2 * (SWEEPS - 1)
    p, q = lax.axis_index("gx"), lax.axis_index("gy")
    source, source_y = field, field_y
    for done in range(1, SWEEPS + 1):
        margin = SWEEPS - done
        start, stop = first - margin, last + margin
        rows, columns = stop - start, brick_x + 2 * margin
        row, skip = start - source_y, SWEEPS - 1 - margin
        here = source[row : row + rows, 1 : 1 + columns, :]
        z = lax.broadcasted_iota(jnp.int32, here.shape, 2)
        total = source[row - 1 : row - 1 + rows, 1 : 1 + columns, :]
        total += source[row + 1 : row + 1 + rows, 1 : 1 + columns, :]
        total += source[row : row + rows, :columns, :]
        total += source[row : row + rows, 2 : 2 + columns, :]
        total += jnp.where(z == 0, 0.0, pltpu.roll(here, 1, 2))
        total += jnp.where(z == points - 1, 0.0, pltpu.roll(here, points - 1, 2))
        row = start - charge_y
        value = (total + charge[row : row + rows, skip : skip + columns, :]) * (1.0 / 6.0)
        if margin == 0:
            return value
        source, source_y = steps[done - 1], start
        source[:rows, :columns, :] = value

        def clear(condition, rows_out, columns_out):
            @pl.when(condition)
            def _():
                part = source[rows_out, columns_out, :]
                source[rows_out, columns_out, :] = jnp.zeros_like(part)

        clear(p == 0, slice(0, rows), slice(0, margin))
        clear(p == sizes[0] - 1, slice(0, rows), slice(margin + brick_x, columns))
        if start < 0:
            clear(q == 0, slice(0, -start), slice(0, columns))
        if stop > brick_y:
            clear(q == sizes[1] - 1, slice(brick_y - start, rows), slice(0, columns))


def lengthen(field_x, charge_x, first, second, field, charge):
    wide, thin = SWEEPS, SWEEPS - 1
    brick_y, width, _ = charge_x.shape
    before, after = sides("gy", first[...], second[...])
    field[:wide, 1 : 1 + width, :] = before[:wide]
    field[wide : wide + brick_y] = field_x[...]
    field[wide + brick_y :, 1 : 1 + width, :] = after[:wide]
    charge[:thin] = before[wide:]
    charge[thin : thin + brick_y] = charge_x[...]
    charge[thin + brick_y :] = after[wide:]


def add_integrals(slots, turned, potential, sums, columns):
    width = sums.shape[1]
    per = turned.shape[2] // width
    empty = sums.shape[0] - 1

    def step(i, carry):
        for x, y in [(2 * i + j, y) for j in range(2) for y in columns]:
            left = turned[x, y]
            weighted = left.astype(jnp.float32) * potential[y, pl.ds(x, 1), :]
            product = lax.dot_general(
                left,
                weighted.astype(turned.dtype),
                (((1,), (1,)), ((), ())),
                preferred_element_type=jnp.float32,
            )
            for a in range(per):
                for b in range(per):
                    slot = slot_of(slots, x, y, a, b, empty)
                    sums[slot] += product[a * width : (a + 1) * width, b * width : (b + 1) * width]
        return carry

    lax.fori_loop(0, turned.shape[0] // 2, step, 0)


def inner_body(sizes, slots, turned, external, field_x, charge_x, _, sums, potential, *steps):
    brick_y = external.shape[0]
    first, last = SWEEPS, brick_y - SWEEPS
    swept = sweeps_in(field_x, 0, charge_x, 0, first, last, brick_y, sizes, steps)
    potential[first:last] = swept + external[first:last]
    add_integrals(slots, turned, potential, sums, range(first, last))


def outer_body(depth, sizes, slots, turned, external, *rest):
    kinds = len(KINDS)
    wide, rest = rest[:4], rest[5:]
    hartree, sums, outs = rest[0], rest[1], rest[2 : 2 + kinds]
    potential, *steps = rest[2 + kinds : 2 + kinds + SWEEPS]
    field, charge, swept, sem = rest[2 + kinds + SWEEPS :]
    brick_y = external.shape[0]
    field[...] = jnp.zeros_like(field)
    lengthen(*wide, field, charge)
    swept[...] = sweeps_in(field, -SWEEPS, charge, 1 - SWEEPS, 0, brick_y, brick_y, sizes, steps)
    copy = pltpu.make_async_copy(swept, hartree, sem)
    copy.start()
    potential[...] = swept[...] + external[...]
    columns = [*range(SWEEPS), *range(brick_y - SWEEPS, brick_y)]
    add_integrals(slots, turned, potential, sums, columns)
    for group, out in zip(group_ids(), outs):
        part = sums[pl.ds(group * depth, depth)]
        out[...] = (CELL_VOLUME * part).astype(out.dtype)
    copy.wait()


def sweep_scratch(brick_y, brick_x, points):
    return [pltpu.VMEM((brick_y, brick_x, points), jnp.float32)] + [
        pltpu.VMEM((brick_y + 2 * margin, 8, points), jnp.float32)
        for margin in range(SWEEPS - 1, 0, -1)
    ]


def integrals_inner(slots, turned, external, field, charge, sums, sizes):
    return call(
        functools.partial(inner_body, sizes),
        "integrals_inner",
        8,
        in_specs=[SMEM] + [VMEM] * 5,
        out_specs=VMEM,
        out_shape=pltpu.VMEM(sums.shape, sums.dtype),
        input_output_aliases={5: 0},
        scratch_shapes=sweep_scratch(*external.shape),
        cost_estimate=cost(turned.size * turned.shape[2]),
    )(slots, turned, external, field, charge, sums)


def integrals_outer(slots, turned, external, wide, sums, depth, sizes):
    kinds = len(KINDS)
    shape = (depth,) + sums.shape[1:]
    brick_y, brick_x, points = external.shape
    return call(
        functools.partial(outer_body, depth, sizes),
        "integrals_outer",
        12,
        in_specs=[SMEM] + [VMEM] * 7,
        out_specs=[ANY] + [VMEM] * (1 + kinds),
        out_shape=[
            jax.ShapeDtypeStruct(external.shape, jnp.float32),
            pltpu.VMEM(sums.shape, sums.dtype),
            jax.ShapeDtypeStruct(shape, jnp.float32),
        ]
        + [jax.ShapeDtypeStruct(shape, jnp.bfloat16)] * (kinds - 1),
        input_output_aliases={7: 1},
        scratch_shapes=sweep_scratch(*external.shape)
        + [
            pltpu.VMEM((brick_y + 2 * SWEEPS, 16, points), jnp.float32),
            pltpu.VMEM((brick_y + 2 * SWEEPS - 2, brick_x + 2 * SWEEPS - 2, points), jnp.float32),
            pltpu.VMEM(external.shape, jnp.float32),
            pltpu.SemaphoreType.DMA,
        ],
        cost_estimate=cost(turned.size * turned.shape[2]),
    )(slots, turned, external, *wide, sums)


def add_blocks(table, messages, kinds, out):
    depth = table.shape[2]
    groups = dict(zip(KINDS, group_ids()))
    for message, kind in zip(messages, kinds):
        for c in range(depth):
            row = table[groups[kind], 0, c]

            @pl.when(row >= 0)
            def _():
                out[row] += message[c].astype(jnp.float32)


def early_body(kinds, table, *rest):
    messages, (total, out, sem) = rest[: len(kinds)], rest[len(kinds) :]
    total[...] = jnp.zeros_like(total)
    add_blocks(table, messages, kinds, total)
    copy = pltpu.make_async_copy(total, out, sem)
    copy.start()
    copy.wait()


def late_body(kinds, table, *rest):
    messages, (_, _, total, out, sems) = rest[: len(kinds)], rest[len(kinds) :]
    add_blocks(table, messages, kinds, total)
    depth = table.shape[2]
    groups = dict(zip(KINDS, group_ids()))
    rows = [table[groups[kind], 0, c] for kind in kinds for c in range(depth)]

    def renewed(i):
        return pltpu.make_async_copy(total.at[rows[i]], out.at[rows[i]], sems.at[i])

    for i, row in enumerate(rows):

        @pl.when(row >= 0)
        def _():
            renewed(i).start()

    for i, row in enumerate(rows):

        @pl.when(row >= 0)
        def _():
            renewed(i).wait()


def collect(table, messages, owned, late=4):
    depth, width, _ = messages[0].shape
    shape = (owned, width, width)
    outs = [pltpu.VMEM(shape, jnp.float32), jax.ShapeDtypeStruct(shape, jnp.float32)]
    early = len(messages) - late
    total, out = call(
        functools.partial(early_body, KINDS[:early]),
        "collect_early",
        4,
        in_specs=[SMEM] + [VMEM] * early,
        out_specs=[VMEM, ANY],
        out_shape=outs,
        scratch_shapes=[pltpu.SemaphoreType.DMA],
        cost_estimate=cost(10**9),
    )(table, *messages[:early])
    return call(
        functools.partial(late_body, KINDS[early:]),
        "collect_late",
        4,
        in_specs=[SMEM] + [VMEM] * (late + 1) + [ANY],
        out_specs=[VMEM, ANY],
        out_shape=outs,
        input_output_aliases={late + 1: 0, late + 2: 1},
        scratch_shapes=[pltpu.SemaphoreType.DMA((late * depth,))],
    )(table, *messages[early:], total, out)[1]


def per_device(
    sizes, density_blocks, send_table, batch_pairs, basis_values, previous_hartree, external_potential
):
    owned, width, _ = density_blocks.shape
    depth = send_table.shape[3]
    table = send_table.reshape(9, 1, depth)
    slots = batch_pairs.transpose(0, 2, 3, 1)
    previous = previous_hartree.transpose(1, 0, 2)
    external = external_potential.transpose(1, 0, 2)
    table_far = pltpu.with_memory_space_constraint(table, pltpu.HBM)
    blocks_far = pltpu.with_memory_space_constraint(density_blocks, pltpu.HBM)
    arrived = spread(gather(table_far, blocks_far), depth, sizes)
    turned = transposed(basis_values, arrived[2])
    to_first, to_second, kept = density_of(slots, turned, previous, arrived, depth)
    second, first = swap(to_second, (2, 0), sizes), swap(to_first, (1, 0), sizes)
    density, sums = copied(kept, (len(KINDS) * depth + 1, width, width))
    field, charge, to_first, to_second = widen(previous, kept, first, second)
    first, second = swap(to_first, (0, 1), sizes), swap(to_second, (0, 2), sizes)
    sums = integrals_inner(slots, turned, external, field, charge, sums, sizes)
    wide = (field, charge, first, second)
    hartree, _, *partial = integrals_outer(slots, turned, external, wide, sums, depth, sizes)
    returned = [partial[0]] + [swap(m, kind, sizes) for m, kind in zip(partial[1:], KINDS[1:])]
    potential = collect(table, returned, owned)
    return density.transpose(1, 0, 2), hartree.transpose(1, 0, 2), potential


def solution(mesh):
    sizes = (mesh.shape["gx"], mesh.shape["gy"])
    in_specs = (
        P(("gx", "gy"), None, None),
        P(("gx", "gy"), None, None, None),
        P("gx", "gy", None, None),
        P("gx", "gy", None, None, None),
        P("gx", "gy", None),
        P("gx", "gy", None),
    )
    out_specs = (P("gx", "gy", None), P("gx", "gy", None), P(("gx", "gy"), None, None))
    return jax.shard_map(
        functools.partial(per_device, sizes),
        mesh=mesh,
        in_specs=in_specs,
        out_specs=out_specs,
        check_vma=False,
    )
```

```python
import functools

import jax
import jax.numpy as jnp
from jax import lax
from jax.experimental import pallas as pl
from jax.experimental.pallas import tpu as pltpu
from jax.sharding import PartitionSpec as P

SWEEPS = 3
CELL_VOLUME = 0.0625

KINDS = ((0, 0), (0, 1), (0, 2), (1, 1), (1, 2), (2, 1), (2, 2), (2, 0), (1, 0))
SENT = (((0, 0),), ((1, 0), (1, 1), (1, 2)), ((0, 1),), ((0, 2),), ((2, 1),), ((2, 2),), ((2, 0),))
ARRIVED = (((0, 0),), ((1, 0),), ((0, 1), (1, 1)), ((0, 2), (1, 2)), ((2, 1),), ((2, 2),), ((2, 0),))


def partner(index, kind):
    if kind == 0:
        return index
    return index + 1 if index % 2 == kind - 1 else index - 1


def swap(value, kind, sizes):
    count_x, count_y = sizes
    pairs = []
    for p in range(count_x):
        for q in range(count_y):
            to_p, to_q = partner(p, kind[0]), partner(q, kind[1])
            if 0 <= to_p < count_x and 0 <= to_q < count_y:
                pairs.append((p * count_y + q, to_p * count_y + to_q))
    return lax.ppermute(value, ("gx", "gy"), pairs)


def group_ids():
    p, q = lax.axis_index("gx"), lax.axis_index("gy")

    def side(index, kind):
        if kind == 0:
            return 1
        return jnp.where((index & 1) == kind - 1, 2, 0)

    return [side(p, a) * 3 + side(q, b) for a, b in KINDS]


def call(body, name, megabytes, **options):
    return pl.pallas_call(
        body,
        name=name,
        compiler_params=pltpu.CompilerParams(vmem_limit_bytes=megabytes * 1024 * 1024),
        **options,
    )


SMEM = pl.BlockSpec(memory_space=pltpu.SMEM)
VMEM = pl.BlockSpec(memory_space=pltpu.VMEM)
ANY = pl.BlockSpec(memory_space=pl.ANY)
HBM = pl.BlockSpec(memory_space=pltpu.HBM)


def gather_body(table_far, blocks_far, *rest):
    outs, (table, blocks, sems) = rest[: len(SENT)], rest[len(SENT) :]
    depth = table.shape[2]
    copies = [
        pltpu.make_async_copy(table_far, table, sems.at[0]),
        pltpu.make_async_copy(blocks_far, blocks, sems.at[1]),
    ]
    for copy in copies:
        copy.start()
    for copy in copies:
        copy.wait()
    groups = dict(zip(KINDS, group_ids()))
    for out, kinds in zip(outs, SENT):
        for part, kind in enumerate(kinds):
            for c in range(depth):
                row = jnp.maximum(table[groups[kind], 0, c], 0)
                out[part * depth + c] = blocks[row]


def gather(table, blocks):
    depth, width = table.shape[2], blocks.shape[1]
    return call(
        gather_body,
        "gather",
        12,
        in_specs=[HBM, HBM],
        out_specs=[VMEM] * len(SENT),
        out_shape=[
            jax.ShapeDtypeStruct((len(kinds) * depth, width, width), blocks.dtype)
            for kinds in SENT
        ],
        scratch_shapes=[
            pltpu.SMEM(table.shape, table.dtype),
            pltpu.VMEM(blocks.shape, blocks.dtype),
            pltpu.SemaphoreType.DMA((2,)),
        ],
    )(table, blocks)


def spread(outgoing, depth, sizes):
    own, to_first, along_first, along_second, *others = outgoing
    first = swap(to_first, (1, 0), sizes)
    one = swap(jnp.concatenate([along_first, first[depth : 2 * depth]]), (0, 1), sizes)
    two = swap(jnp.concatenate([along_second, first[2 * depth :]]), (0, 2), sizes)
    rest = [swap(blocks, kinds[0], sizes) for blocks, kinds in zip(others, SENT[4:])]
    return [own, first, one, two, *rest]


def transpose_body(basis, after, turned, held, sems):
    brick_x, brick_y, per, _, width = basis.shape
    half = brick_y // 2
    parts = [(x, j) for x in range(brick_x) for j in range(2)]

    def coming(i):
        x, j = parts[i]
        here = pl.ds(j * half, half)
        return pltpu.make_async_copy(basis.at[x, here], held.at[x, here], sems.at[i])

    for i in range(len(parts)):
        coming(i).start()
    for i, (x, j) in enumerate(parts):
        coming(i).wait()
        for y in range(j * half, (j + 1) * half):
            for b in range(per):
                turned[x, y, b * width : (b + 1) * width, :] = held[x, y, b].T


def transposed(basis, after):
    brick_x, brick_y, per, points, width = basis.shape
    return call(
        transpose_body,
        "transpose",
        32,
        in_specs=[ANY, ANY],
        out_specs=VMEM,
        out_shape=pltpu.VMEM((brick_x, brick_y, per * width, points), basis.dtype),
        scratch_shapes=[
            pltpu.VMEM(basis.shape, basis.dtype),
            pltpu.SemaphoreType.DMA((2 * brick_x,)),
        ],
        cost_estimate=pl.CostEstimate(flops=0, bytes_accessed=4 * basis.size, transcendentals=0),
    )(basis, after)


def slot_of(slots, x, y, a, b, empty):
    slot = slots[x, a, b, y]
    return jnp.where(slot < 0, empty, slot)


def message_of(out, previous, density, low):
    brick_y, brick_x, _ = previous.shape
    thin = SWEEPS - 1
    out[:brick_y] = previous[...]
    per = brick_x // thin
    for y in range(brick_y):
        layers = jnp.where(low, density[y, :thin, :], density[y, brick_x - thin :, :])
        out[brick_y + y // per, (y % per) * thin : (y % per + 1) * thin, :] = layers


def density_body(depth, slots, turned, previous, *rest):
    arrived, (to_first, to_second, kept, flat, blocks) = rest[: len(ARRIVED)], rest[len(ARRIVED) :]
    brick_x, brick_y, rows, _ = turned.shape
    width = blocks.shape[1]
    per = rows // width
    empty = len(KINDS) * depth
    groups = dict(zip(KINDS, group_ids()))
    for message, kinds in zip(arrived, ARRIVED):
        for part, kind in enumerate(kinds):
            blocks[pl.ds(groups[kind] * depth, depth)] = message[part * depth : (part + 1) * depth]
    blocks[empty] = jnp.zeros((width, width), blocks.dtype)

    def step(x, carry):
        for y in range(brick_y):
            used = [slot_of(slots, x, y, i // per, i % per, empty) for i in range(per * per)]
            for i, slot in enumerate(used):
                flat[(x * brick_y + y) * per * per + i] = slot
            lefts = [
                jnp.concatenate([blocks[slot] for slot in used[a * per : (a + 1) * per]], axis=1)
                for a in range(per)
            ]
            right = turned[x, y]
            mixed = jnp.dot(
                jnp.concatenate(lefts, axis=0), right, preferred_element_type=jnp.float32
            )
            product = mixed * right.astype(jnp.float32)
            kept[y, pl.ds(x, 1), :] = jnp.sum(product, axis=0, keepdims=True)
        return carry

    lax.fori_loop(0, brick_x, step, 0)
    odd = (lax.axis_index("gx") & 1) == 1
    message_of(to_first, previous, kept, odd)
    message_of(to_second, previous, kept, jnp.logical_not(odd))


def density_of(slots, turned, previous, arrived, depth):
    brick_x, brick_y, rows, points = turned.shape
    width = arrived[0].shape[1]
    thin = SWEEPS - 1
    shape = (brick_y, brick_x, points)
    message = jax.ShapeDtypeStruct((brick_y + brick_y * thin // brick_x, brick_x, points), jnp.float32)
    return call(
        functools.partial(density_body, depth),
        "density",
        12,
        in_specs=[SMEM] + [VMEM] * (2 + len(arrived)),
        out_specs=[VMEM] * 3 + [SMEM],
        out_shape=[message, message, jax.ShapeDtypeStruct(shape, jnp.float32)]
        + [jax.ShapeDtypeStruct((brick_x * brick_y * (rows // width) ** 2,), jnp.int32)],
        scratch_shapes=[pltpu.VMEM((len(KINDS) * depth + 1, width, width), turned.dtype)],
    )(slots, turned, previous, *arrived)


def copied_body(kept, density, sums):
    density[...] = kept[...]
    sums[...] = jnp.zeros_like(sums)


def copied(kept, shape):
    return call(
        copied_body,
        "copied",
        4,
        in_specs=[VMEM],
        out_specs=[VMEM] * 2,
        out_shape=[jax.ShapeDtypeStruct(kept.shape, kept.dtype), pltpu.VMEM(shape, jnp.float32)],
    )(kept)


def cost(flops):
    return pl.CostEstimate(flops=flops, bytes_accessed=0, transcendentals=0)


def sides(axis, first, second):
    even = (lax.axis_index(axis) & 1) == 0
    return jnp.where(even, second, first), jnp.where(even, first, second)


def widen_body(previous, density, first, second, field, charge, to_first, to_second):
    wide, thin = SWEEPS, SWEEPS - 1
    brick_y, brick_x, points = density.shape
    per = brick_x // thin
    before, after = sides("gx", first[...], second[...])
    field[...] = jnp.zeros_like(field)
    field[:, :wide, :] = before[:brick_y, brick_x - wide :, :]
    field[:, wide : wide + brick_x, :] = previous[...]
    field[:, wide + brick_x : 2 * wide + brick_x, :] = after[:brick_y, :wide, :]
    charge[:, thin : thin + brick_x, :] = density[...]
    for y in range(brick_y):
        row, start = brick_y + y // per, (y % per) * thin
        charge[y, :thin, :] = before[row, start : start + thin, :]
        charge[y, thin + brick_x :, :] = after[row, start : start + thin, :]
    width = brick_x + 2 * thin
    even = (lax.axis_index("gy") & 1) == 0
    low = [field[:wide, 1 : 1 + width, :], charge[:thin]]
    high = [field[brick_y - wide :, 1 : 1 + width, :], charge[brick_y - thin :]]
    for out, where_even, where_odd in ((to_first, high, low), (to_second, low, high)):
        out[:wide] = jnp.where(even, where_even[0], where_odd[0])
        out[wide:] = jnp.where(even, where_even[1], where_odd[1])


def widen(previous, density, first, second):
    brick_y, brick_x, points = density.shape
    wide, thin = SWEEPS, SWEEPS - 1
    width = brick_x + 2 * thin
    shapes = [(brick_y, 16, points), (brick_y, width, points)] + [(wide + thin, width, points)] * 2
    return call(
        widen_body,
        "widen",
        4,
        in_specs=[VMEM] * 4,
        out_specs=[VMEM] * 4,
        out_shape=[jax.ShapeDtypeStruct(shape, jnp.float32) for shape in shapes],
    )(previous, density, first, second)


def sweeps_in(field, field_y, charge, charge_y, first, last, brick_y, sizes, steps):
    points = field.shape[2]
    brick_x = charge.shape[1] - 2 * (SWEEPS - 1)
    p, q = lax.axis_index("gx"), lax.axis_index("gy")
    source, source_y = field, field_y
    for done in range(1, SWEEPS + 1):
        margin = SWEEPS - done
        start, stop = first - margin, last + margin
        rows, columns = stop - start, brick_x + 2 * margin
        row, skip = start - source_y, SWEEPS - 1 - margin
        here = source[row : row + rows, 1 : 1 + columns, :]
        z = lax.broadcasted_iota(jnp.int32, here.shape, 2)
        total = source[row - 1 : row - 1 + rows, 1 : 1 + columns, :]
        total += source[row + 1 : row + 1 + rows, 1 : 1 + columns, :]
        total += source[row : row + rows, :columns, :]
        total += source[row : row + rows, 2 : 2 + columns, :]
        total += jnp.where(z == 0, 0.0, pltpu.roll(here, 1, 2))
        total += jnp.where(z == points - 1, 0.0, pltpu.roll(here, points - 1, 2))
        row = start - charge_y
        value = (total + charge[row : row + rows, skip : skip + columns, :]) * (1.0 / 6.0)
        if margin == 0:
            return value
        source, source_y = steps[done - 1], start
        source[:rows, :columns, :] = value

        def clear(condition, rows_out, columns_out):
            @pl.when(condition)
            def _():
                part = source[rows_out, columns_out, :]
                source[rows_out, columns_out, :] = jnp.zeros_like(part)

        clear(p == 0, slice(0, rows), slice(0, margin))
        clear(p == sizes[0] - 1, slice(0, rows), slice(margin + brick_x, columns))
        if start < 0:
            clear(q == 0, slice(0, -start), slice(0, columns))
        if stop > brick_y:
            clear(q == sizes[1] - 1, slice(brick_y - start, rows), slice(0, columns))


def lengthen(field_x, charge_x, first, second, field, charge):
    wide, thin = SWEEPS, SWEEPS - 1
    brick_y, width, _ = charge_x.shape
    before, after = sides("gy", first[...], second[...])
    field[:wide, 1 : 1 + width, :] = before[:wide]
    field[wide : wide + brick_y] = field_x[...]
    field[wide + brick_y :, 1 : 1 + width, :] = after[:wide]
    charge[:thin] = before[wide:]
    charge[thin : thin + brick_y] = charge_x[...]
    charge[thin + brick_y :] = after[wide:]


def add_integrals(slots, turned, potential, sums, columns):
    width = sums.shape[1]
    per = turned.shape[2] // width
    brick_y = turned.shape[1]

    def step(i, carry):
        for x, y in [(2 * i + j, y) for j in range(2) for y in columns]:
            left = turned[x, y]
            weighted = left.astype(jnp.float32) * potential[y, pl.ds(x, 1), :]
            product = lax.dot_general(
                left,
                weighted.astype(turned.dtype),
                (((1,), (1,)), ((), ())),
                preferred_element_type=jnp.float32,
            )
            for a in range(per):
                for b in range(per):
                    slot = slots[(x * brick_y + y) * per * per + a * per + b]
                    sums[slot] += product[a * width : (a + 1) * width, b * width : (b + 1) * width]
        return carry

    lax.fori_loop(0, turned.shape[0] // 2, step, 0)


def inner_body(sizes, slots, turned, external, field_x, charge_x, _, sums, potential, *steps):
    brick_y = external.shape[0]
    first, last = SWEEPS, brick_y - SWEEPS
    swept = sweeps_in(field_x, 0, charge_x, 0, first, last, brick_y, sizes, steps)
    potential[first:last] = swept + external[first:last]
    add_integrals(slots, turned, potential, sums, range(first, last))


def outer_body(depth, sizes, slots, turned, external, *rest):
    kinds = len(KINDS)
    wide, rest = rest[:4], rest[5:]
    hartree, sums, outs = rest[0], rest[1], rest[2 : 2 + kinds]
    potential, *steps = rest[2 + kinds : 2 + kinds + SWEEPS]
    field, charge, swept, sem = rest[2 + kinds + SWEEPS :]
    brick_y = external.shape[0]
    field[...] = jnp.zeros_like(field)
    lengthen(*wide, field, charge)
    swept[...] = sweeps_in(field, -SWEEPS, charge, 1 - SWEEPS, 0, brick_y, brick_y, sizes, steps)
    copy = pltpu.make_async_copy(swept, hartree, sem)
    copy.start()
    potential[...] = swept[...] + external[...]
    columns = [*range(SWEEPS), *range(brick_y - SWEEPS, brick_y)]
    add_integrals(slots, turned, potential, sums, columns)
    for group, out in zip(group_ids(), outs):
        part = sums[pl.ds(group * depth, depth)]
        out[...] = (CELL_VOLUME * part).astype(out.dtype)
    copy.wait()


def sweep_scratch(brick_y, brick_x, points):
    return [pltpu.VMEM((brick_y, brick_x, points), jnp.float32)] + [
        pltpu.VMEM((brick_y + 2 * margin, 8, points), jnp.float32)
        for margin in range(SWEEPS - 1, 0, -1)
    ]


def integrals_inner(slots, turned, external, field, charge, sums, sizes):
    return call(
        functools.partial(inner_body, sizes),
        "integrals_inner",
        8,
        in_specs=[SMEM] + [VMEM] * 5,
        out_specs=VMEM,
        out_shape=pltpu.VMEM(sums.shape, sums.dtype),
        input_output_aliases={5: 0},
        scratch_shapes=sweep_scratch(*external.shape),
        cost_estimate=cost(turned.size * turned.shape[2]),
    )(slots, turned, external, field, charge, sums)


def integrals_outer(slots, turned, external, wide, sums, depth, sizes):
    kinds = len(KINDS)
    shape = (depth,) + sums.shape[1:]
    brick_y, brick_x, points = external.shape
    return call(
        functools.partial(outer_body, depth, sizes),
        "integrals_outer",
        12,
        in_specs=[SMEM] + [VMEM] * 7,
        out_specs=[ANY] + [VMEM] * (1 + kinds),
        out_shape=[
            jax.ShapeDtypeStruct(external.shape, jnp.float32),
            pltpu.VMEM(sums.shape, sums.dtype),
            jax.ShapeDtypeStruct(shape, jnp.float32),
        ]
        + [jax.ShapeDtypeStruct(shape, jnp.bfloat16)] * (kinds - 1),
        input_output_aliases={7: 1},
        scratch_shapes=sweep_scratch(*external.shape)
        + [
            pltpu.VMEM((brick_y + 2 * SWEEPS, 16, points), jnp.float32),
            pltpu.VMEM((brick_y + 2 * SWEEPS - 2, brick_x + 2 * SWEEPS - 2, points), jnp.float32),
            pltpu.VMEM(external.shape, jnp.float32),
            pltpu.SemaphoreType.DMA,
        ],
        cost_estimate=cost(turned.size * turned.shape[2]),
    )(slots, turned, external, *wide, sums)


def add_blocks(table, messages, kinds, out):
    depth = table.shape[2]
    groups = dict(zip(KINDS, group_ids()))
    for message, kind in zip(messages, kinds):
        for c in range(depth):
            row = table[groups[kind], 0, c]

            @pl.when(row >= 0)
            def _():
                out[row] += message[c].astype(jnp.float32)


def early_body(kinds, table, *rest):
    messages, (total, out, sem) = rest[: len(kinds)], rest[len(kinds) :]
    total[...] = jnp.zeros_like(total)
    add_blocks(table, messages, kinds, total)
    copy = pltpu.make_async_copy(total, out, sem)
    copy.start()
    copy.wait()


def late_body(kinds, table, *rest):
    messages, (_, _, total, out, sems) = rest[: len(kinds)], rest[len(kinds) :]
    add_blocks(table, messages, kinds, total)
    depth = table.shape[2]
    groups = dict(zip(KINDS, group_ids()))
    rows = [table[groups[kind], 0, c] for kind in kinds for c in range(depth)]

    def renewed(i):
        return pltpu.make_async_copy(total.at[rows[i]], out.at[rows[i]], sems.at[i])

    for i, row in enumerate(rows):

        @pl.when(row >= 0)
        def _():
            renewed(i).start()

    for i, row in enumerate(rows):

        @pl.when(row >= 0)
        def _():
            renewed(i).wait()


def collect(table, messages, owned, late=4):
    depth, width, _ = messages[0].shape
    shape = (owned, width, width)
    outs = [pltpu.VMEM(shape, jnp.float32), jax.ShapeDtypeStruct(shape, jnp.float32)]
    early = len(messages) - late
    total, out = call(
        functools.partial(early_body, KINDS[:early]),
        "collect_early",
        4,
        in_specs=[SMEM] + [VMEM] * early,
        out_specs=[VMEM, ANY],
        out_shape=outs,
        scratch_shapes=[pltpu.SemaphoreType.DMA],
        cost_estimate=cost(10**9),
    )(table, *messages[:early])
    return call(
        functools.partial(late_body, KINDS[early:]),
        "collect_late",
        4,
        in_specs=[SMEM] + [VMEM] * (late + 1) + [ANY],
        out_specs=[VMEM, ANY],
        out_shape=outs,
        input_output_aliases={late + 1: 0, late + 2: 1},
        scratch_shapes=[pltpu.SemaphoreType.DMA((late * depth,))],
    )(table, *messages[early:], total, out)[1]


def per_device(
    sizes, density_blocks, send_table, batch_pairs, basis_values, previous_hartree, external_potential
):
    owned, width, _ = density_blocks.shape
    depth = send_table.shape[3]
    table = send_table.reshape(9, 1, depth)
    slots = batch_pairs.transpose(0, 2, 3, 1)
    previous = previous_hartree.transpose(1, 0, 2)
    external = external_potential.transpose(1, 0, 2)
    table_far = pltpu.with_memory_space_constraint(table, pltpu.HBM)
    blocks_far = pltpu.with_memory_space_constraint(density_blocks, pltpu.HBM)
    arrived = spread(gather(table_far, blocks_far), depth, sizes)
    turned = transposed(basis_values, arrived[1])
    to_first, to_second, kept, flat = density_of(slots, turned, previous, arrived, depth)
    second, first = swap(to_second, (2, 0), sizes), swap(to_first, (1, 0), sizes)
    density, sums = copied(kept, (len(KINDS) * depth + 1, width, width))
    field, charge, to_first, to_second = widen(previous, kept, first, second)
    first, second = swap(to_first, (0, 1), sizes), swap(to_second, (0, 2), sizes)
    sums = integrals_inner(flat, turned, external, field, charge, sums, sizes)
    wide = (field, charge, first, second)
    hartree, _, *partial = integrals_outer(flat, turned, external, wide, sums, depth, sizes)
    returned = [partial[0]] + [swap(m, kind, sizes) for m, kind in zip(partial[1:], KINDS[1:])]
    potential = collect(table, returned, owned)
    return density.transpose(1, 0, 2), hartree.transpose(1, 0, 2), potential


def solution(mesh):
    sizes = (mesh.shape["gx"], mesh.shape["gy"])
    in_specs = (
        P(("gx", "gy"), None, None),
        P(("gx", "gy"), None, None, None),
        P("gx", "gy", None, None),
        P("gx", "gy", None, None, None),
        P("gx", "gy", None),
        P("gx", "gy", None),
    )
    out_specs = (P("gx", "gy", None), P("gx", "gy", None), P(("gx", "gy"), None, None))
    return jax.shard_map(
        functools.partial(per_device, sizes),
        mesh=mesh,
        in_specs=in_specs,
        out_specs=out_specs,
        check_vma=False,
    )
```

```python
import functools

import jax
import jax.numpy as jnp
from jax import lax
from jax.experimental import pallas as pl
from jax.experimental.pallas import tpu as pltpu
from jax.sharding import PartitionSpec as P

SWEEPS = 3
CELL_VOLUME = 0.0625

KINDS = ((0, 0), (0, 1), (0, 2), (1, 1), (1, 2), (2, 1), (2, 2), (2, 0), (1, 0))
SENT = (((0, 0),), ((1, 0), (1, 1), (1, 2)), ((0, 1),), ((0, 2),), ((2, 1),), ((2, 2),), ((2, 0),))
ARRIVED = (((0, 0),), ((1, 0),), ((0, 1), (1, 1)), ((0, 2), (1, 2)), ((2, 1),), ((2, 2),), ((2, 0),))


def partner(index, kind):
    if kind == 0:
        return index
    return index + 1 if index % 2 == kind - 1 else index - 1


def swap(value, kind, sizes):
    count_x, count_y = sizes
    pairs = []
    for p in range(count_x):
        for q in range(count_y):
            to_p, to_q = partner(p, kind[0]), partner(q, kind[1])
            if 0 <= to_p < count_x and 0 <= to_q < count_y:
                pairs.append((p * count_y + q, to_p * count_y + to_q))
    return lax.ppermute(value, ("gx", "gy"), pairs)


def group_ids():
    p, q = lax.axis_index("gx"), lax.axis_index("gy")

    def side(index, kind):
        if kind == 0:
            return 1
        return jnp.where((index & 1) == kind - 1, 2, 0)

    return [side(p, a) * 3 + side(q, b) for a, b in KINDS]


def call(body, name, megabytes, **options):
    return pl.pallas_call(
        body,
        name=name,
        compiler_params=pltpu.CompilerParams(vmem_limit_bytes=megabytes * 1024 * 1024),
        **options,
    )


SMEM = pl.BlockSpec(memory_space=pltpu.SMEM)
VMEM = pl.BlockSpec(memory_space=pltpu.VMEM)
ANY = pl.BlockSpec(memory_space=pl.ANY)
HBM = pl.BlockSpec(memory_space=pltpu.HBM)


def gather_body(table_far, blocks_far, *rest):
    outs, (table, blocks, sems) = rest[: len(SENT)], rest[len(SENT) :]
    depth = table.shape[2]
    copies = [
        pltpu.make_async_copy(table_far, table, sems.at[0]),
        pltpu.make_async_copy(blocks_far, blocks, sems.at[1]),
    ]
    for copy in copies:
        copy.start()
    for copy in copies:
        copy.wait()
    groups = dict(zip(KINDS, group_ids()))
    for out, kinds in zip(outs, SENT):
        for part, kind in enumerate(kinds):
            for c in range(depth):
                row = jnp.maximum(table[groups[kind], 0, c], 0)
                out[part * depth + c] = blocks[row]


def gather(table, blocks):
    depth, width = table.shape[2], blocks.shape[1]
    return call(
        gather_body,
        "gather",
        12,
        in_specs=[HBM, HBM],
        out_specs=[VMEM] * len(SENT),
        out_shape=[
            jax.ShapeDtypeStruct((len(kinds) * depth, width, width), blocks.dtype)
            for kinds in SENT
        ],
        scratch_shapes=[
            pltpu.SMEM(table.shape, table.dtype),
            pltpu.VMEM(blocks.shape, blocks.dtype),
            pltpu.SemaphoreType.DMA((2,)),
        ],
    )(table, blocks)


def spread(outgoing, depth, sizes):
    own, to_first, along_first, along_second, *others = outgoing
    first = swap(to_first, (1, 0), sizes)
    one = swap(jnp.concatenate([along_first, first[depth : 2 * depth]]), (0, 1), sizes)
    two = swap(jnp.concatenate([along_second, first[2 * depth :]]), (0, 2), sizes)
    rest = [swap(blocks, kinds[0], sizes) for blocks, kinds in zip(others, SENT[4:])]
    return [own, first, one, two, *rest]


def transpose_body(empty, basis, after, slots, turned, flat, held, sems):
    brick_x, brick_y, per, _, width = basis.shape
    half = brick_y // 2
    parts = [(x, j) for x in range(brick_x) for j in range(2)]

    def coming(i):
        x, j = parts[i]
        here = pl.ds(j * half, half)
        return pltpu.make_async_copy(basis.at[x, here], held.at[x, here], sems.at[i])

    for i in range(len(parts)):
        coming(i).start()
    for i, (x, j) in enumerate(parts):
        coming(i).wait()
        for y in range(j * half, (j + 1) * half):
            for b in range(per):
                turned[x, y, b * width : (b + 1) * width, :] = held[x, y, b].T
            for pair in range(per * per):
                slot = slots[x, pair // per, pair % per, y]
                flat[(x * brick_y + y) * per * per + pair] = jnp.where(slot < 0, empty, slot)


def transposed(basis, after, slots, empty):
    brick_x, brick_y, per, points, width = basis.shape
    return call(
        functools.partial(transpose_body, empty),
        "transpose",
        32,
        in_specs=[ANY, ANY, SMEM],
        out_specs=[VMEM, SMEM],
        out_shape=[
            jax.ShapeDtypeStruct((brick_x, brick_y, per * width, points), basis.dtype),
            jax.ShapeDtypeStruct((brick_x * brick_y * per * per,), jnp.int32),
        ],
        scratch_shapes=[
            pltpu.VMEM(basis.shape, basis.dtype),
            pltpu.SemaphoreType.DMA((2 * brick_x,)),
        ],
        cost_estimate=pl.CostEstimate(flops=0, bytes_accessed=4 * basis.size, transcendentals=0),
    )(basis, after, slots)


def message_of(out, previous, density, low):
    brick_y, brick_x, _ = previous.shape
    thin = SWEEPS - 1
    out[:brick_y] = previous[...]
    per = brick_x // thin
    for y in range(brick_y):
        layers = jnp.where(low, density[y, :thin, :], density[y, brick_x - thin :, :])
        out[brick_y + y // per, (y % per) * thin : (y % per + 1) * thin, :] = layers


def density_body(depth, slots, turned, previous, *rest):
    arrived, (to_first, to_second, kept, blocks) = rest[: len(ARRIVED)], rest[len(ARRIVED) :]
    brick_x, brick_y, rows, _ = turned.shape
    width = blocks.shape[1]
    per = rows // width
    empty = len(KINDS) * depth
    groups = dict(zip(KINDS, group_ids()))
    for message, kinds in zip(arrived, ARRIVED):
        for part, kind in enumerate(kinds):
            blocks[pl.ds(groups[kind] * depth, depth)] = message[part * depth : (part + 1) * depth]
    blocks[empty] = jnp.zeros((width, width), blocks.dtype)

    def step(x, carry):
        for y in range(brick_y):
            used = [slots[(x * brick_y + y) * per * per + i] for i in range(per * per)]
            lefts = [
                jnp.concatenate([blocks[slot] for slot in used[a * per : (a + 1) * per]], axis=1)
                for a in range(per)
            ]
            right = turned[x, y]
            mixed = jnp.dot(
                jnp.concatenate(lefts, axis=0), right, preferred_element_type=jnp.float32
            )
            product = mixed * right.astype(jnp.float32)
            kept[y, pl.ds(x, 1), :] = jnp.sum(product, axis=0, keepdims=True)
        return carry

    lax.fori_loop(0, brick_x, step, 0)
    odd = (lax.axis_index("gx") & 1) == 1
    message_of(to_first, previous, kept, odd)
    message_of(to_second, previous, kept, jnp.logical_not(odd))


def density_of(slots, turned, previous, arrived, depth):
    brick_x, brick_y, rows, points = turned.shape
    width = arrived[0].shape[1]
    thin = SWEEPS - 1
    shape = (brick_y, brick_x, points)
    message = jax.ShapeDtypeStruct((brick_y + brick_y * thin // brick_x, brick_x, points), jnp.float32)
    return call(
        functools.partial(density_body, depth),
        "density",
        12,
        in_specs=[SMEM] + [VMEM] * (2 + len(arrived)),
        out_specs=[VMEM] * 3,
        out_shape=[message, message, jax.ShapeDtypeStruct(shape, jnp.float32)],
        scratch_shapes=[pltpu.VMEM((len(KINDS) * depth + 1, width, width), turned.dtype)],
    )(slots, turned, previous, *arrived)


def copied_body(kept, density, sums):
    density[...] = kept[...]
    sums[...] = jnp.zeros_like(sums)


def copied(kept, shape):
    return call(
        copied_body,
        "copied",
        4,
        in_specs=[VMEM],
        out_specs=[VMEM] * 2,
        out_shape=[jax.ShapeDtypeStruct(kept.shape, kept.dtype), pltpu.VMEM(shape, jnp.float32)],
    )(kept)


def cost(flops):
    return pl.CostEstimate(flops=flops, bytes_accessed=0, transcendentals=0)


def sides(axis, first, second):
    even = (lax.axis_index(axis) & 1) == 0
    return jnp.where(even, second, first), jnp.where(even, first, second)


def widen_body(previous, density, first, second, field, charge, to_first, to_second):
    wide, thin = SWEEPS, SWEEPS - 1
    brick_y, brick_x, points = density.shape
    per = brick_x // thin
    before, after = sides("gx", first[...], second[...])
    field[...] = jnp.zeros_like(field)
    field[:, :wide, :] = before[:brick_y, brick_x - wide :, :]
    field[:, wide : wide + brick_x, :] = previous[...]
    field[:, wide + brick_x : 2 * wide + brick_x, :] = after[:brick_y, :wide, :]
    charge[:, thin : thin + brick_x, :] = density[...]
    for y in range(brick_y):
        row, start = brick_y + y // per, (y % per) * thin
        charge[y, :thin, :] = before[row, start : start + thin, :]
        charge[y, thin + brick_x :, :] = after[row, start : start + thin, :]
    width = brick_x + 2 * thin
    even = (lax.axis_index("gy") & 1) == 0
    low = [field[:wide, 1 : 1 + width, :], charge[:thin]]
    high = [field[brick_y - wide :, 1 : 1 + width, :], charge[brick_y - thin :]]
    for out, where_even, where_odd in ((to_first, high, low), (to_second, low, high)):
        out[:wide] = jnp.where(even, where_even[0], where_odd[0])
        out[wide:] = jnp.where(even, where_even[1], where_odd[1])


def widen(previous, density, first, second):
    brick_y, brick_x, points = density.shape
    wide, thin = SWEEPS, SWEEPS - 1
    width = brick_x + 2 * thin
    shapes = [(brick_y, 16, points), (brick_y, width, points)] + [(wide + thin, width, points)] * 2
    return call(
        widen_body,
        "widen",
        4,
        in_specs=[VMEM] * 4,
        out_specs=[VMEM] * 4,
        out_shape=[jax.ShapeDtypeStruct(shape, jnp.float32) for shape in shapes],
    )(previous, density, first, second)


def sweeps_in(field, field_y, charge, charge_y, first, last, brick_y, sizes, steps):
    points = field.shape[2]
    brick_x = charge.shape[1] - 2 * (SWEEPS - 1)
    p, q = lax.axis_index("gx"), lax.axis_index("gy")
    source, source_y = field, field_y
    for done in range(1, SWEEPS + 1):
        margin = SWEEPS - done
        start, stop = first - margin, last + margin
        rows, columns = stop - start, brick_x + 2 * margin
        row, skip = start - source_y, SWEEPS - 1 - margin
        here = source[row : row + rows, 1 : 1 + columns, :]
        z = lax.broadcasted_iota(jnp.int32, here.shape, 2)
        total = source[row - 1 : row - 1 + rows, 1 : 1 + columns, :]
        total += source[row + 1 : row + 1 + rows, 1 : 1 + columns, :]
        total += source[row : row + rows, :columns, :]
        total += source[row : row + rows, 2 : 2 + columns, :]
        total += jnp.where(z == 0, 0.0, pltpu.roll(here, 1, 2))
        total += jnp.where(z == points - 1, 0.0, pltpu.roll(here, points - 1, 2))
        row = start - charge_y
        value = (total + charge[row : row + rows, skip : skip + columns, :]) * (1.0 / 6.0)
        if margin == 0:
            return value
        source, source_y = steps[done - 1], start
        source[:rows, :columns, :] = value

        def clear(condition, rows_out, columns_out):
            @pl.when(condition)
            def _():
                part = source[rows_out, columns_out, :]
                source[rows_out, columns_out, :] = jnp.zeros_like(part)

        clear(p == 0, slice(0, rows), slice(0, margin))
        clear(p == sizes[0] - 1, slice(0, rows), slice(margin + brick_x, columns))
        if start < 0:
            clear(q == 0, slice(0, -start), slice(0, columns))
        if stop > brick_y:
            clear(q == sizes[1] - 1, slice(brick_y - start, rows), slice(0, columns))


def lengthen(field_x, charge_x, first, second, field, charge):
    wide, thin = SWEEPS, SWEEPS - 1
    brick_y, width, _ = charge_x.shape
    before, after = sides("gy", first[...], second[...])
    field[:wide, 1 : 1 + width, :] = before[:wide]
    field[wide : wide + brick_y] = field_x[...]
    field[wide + brick_y :, 1 : 1 + width, :] = after[:wide]
    charge[:thin] = before[wide:]
    charge[thin : thin + brick_y] = charge_x[...]
    charge[thin + brick_y :] = after[wide:]


def add_integrals(slots, turned, potential, sums, columns):
    width = sums.shape[1]
    per = turned.shape[2] // width
    brick_y = turned.shape[1]

    def step(i, carry):
        for x, y in [(2 * i + j, y) for j in range(2) for y in columns]:
            left = turned[x, y]
            weighted = left.astype(jnp.float32) * potential[y, pl.ds(x, 1), :]
            product = lax.dot_general(
                left,
                weighted.astype(turned.dtype),
                (((1,), (1,)), ((), ())),
                preferred_element_type=jnp.float32,
            )
            for a in range(per):
                for b in range(per):
                    slot = slots[(x * brick_y + y) * per * per + a * per + b]
                    sums[slot] += product[a * width : (a + 1) * width, b * width : (b + 1) * width]
        return carry

    lax.fori_loop(0, turned.shape[0] // 2, step, 0)


def inner_body(sizes, slots, turned, external, field_x, charge_x, _, sums, potential, *steps):
    brick_y = external.shape[0]
    first, last = SWEEPS, brick_y - SWEEPS
    swept = sweeps_in(field_x, 0, charge_x, 0, first, last, brick_y, sizes, steps)
    potential[first:last] = swept + external[first:last]
    add_integrals(slots, turned, potential, sums, range(first, last))


def outer_body(depth, sizes, slots, turned, external, *rest):
    kinds = len(KINDS)
    wide, rest = rest[:4], rest[5:]
    hartree, sums, outs = rest[0], rest[1], rest[2 : 2 + kinds]
    potential, *steps = rest[2 + kinds : 2 + kinds + SWEEPS]
    field, charge, swept, sem = rest[2 + kinds + SWEEPS :]
    brick_y = external.shape[0]
    field[...] = jnp.zeros_like(field)
    lengthen(*wide, field, charge)
    swept[...] = sweeps_in(field, -SWEEPS, charge, 1 - SWEEPS, 0, brick_y, brick_y, sizes, steps)
    copy = pltpu.make_async_copy(swept, hartree, sem)
    copy.start()
    potential[...] = swept[...] + external[...]
    columns = [*range(SWEEPS), *range(brick_y - SWEEPS, brick_y)]
    add_integrals(slots, turned, potential, sums, columns)
    for group, out in zip(group_ids(), outs):
        part = sums[pl.ds(group * depth, depth)]
        out[...] = (CELL_VOLUME * part).astype(out.dtype)
    copy.wait()


def sweep_scratch(brick_y, brick_x, points):
    return [pltpu.VMEM((brick_y, brick_x, points), jnp.float32)] + [
        pltpu.VMEM((brick_y + 2 * margin, 8, points), jnp.float32)
        for margin in range(SWEEPS - 1, 0, -1)
    ]


def integrals_inner(slots, turned, external, field, charge, sums, sizes):
    return call(
        functools.partial(inner_body, sizes),
        "integrals_inner",
        8,
        in_specs=[SMEM] + [VMEM] * 5,
        out_specs=VMEM,
        out_shape=pltpu.VMEM(sums.shape, sums.dtype),
        input_output_aliases={5: 0},
        scratch_shapes=sweep_scratch(*external.shape),
        cost_estimate=cost(turned.size * turned.shape[2]),
    )(slots, turned, external, field, charge, sums)


def integrals_outer(slots, turned, external, wide, sums, depth, sizes):
    kinds = len(KINDS)
    shape = (depth,) + sums.shape[1:]
    brick_y, brick_x, points = external.shape
    return call(
        functools.partial(outer_body, depth, sizes),
        "integrals_outer",
        12,
        in_specs=[SMEM] + [VMEM] * 7,
        out_specs=[ANY] + [VMEM] * (1 + kinds),
        out_shape=[
            jax.ShapeDtypeStruct(external.shape, jnp.float32),
            pltpu.VMEM(sums.shape, sums.dtype),
            jax.ShapeDtypeStruct(shape, jnp.float32),
        ]
        + [jax.ShapeDtypeStruct(shape, jnp.bfloat16)] * (kinds - 1),
        input_output_aliases={7: 1},
        scratch_shapes=sweep_scratch(*external.shape)
        + [
            pltpu.VMEM((brick_y + 2 * SWEEPS, 16, points), jnp.float32),
            pltpu.VMEM((brick_y + 2 * SWEEPS - 2, brick_x + 2 * SWEEPS - 2, points), jnp.float32),
            pltpu.VMEM(external.shape, jnp.float32),
            pltpu.SemaphoreType.DMA,
        ],
        cost_estimate=cost(turned.size * turned.shape[2]),
    )(slots, turned, external, *wide, sums)


def add_blocks(table, messages, kinds, out):
    depth = table.shape[2]
    groups = dict(zip(KINDS, group_ids()))
    for message, kind in zip(messages, kinds):
        for c in range(depth):
            row = table[groups[kind], 0, c]

            @pl.when(row >= 0)
            def _():
                out[row] += message[c].astype(jnp.float32)


def early_body(kinds, table, *rest):
    messages, (total, out, sem) = rest[: len(kinds)], rest[len(kinds) :]
    total[...] = jnp.zeros_like(total)
    add_blocks(table, messages, kinds, total)
    copy = pltpu.make_async_copy(total, out, sem)
    copy.start()
    copy.wait()


def late_body(kinds, table, *rest):
    messages, (_, _, total, out, sems) = rest[: len(kinds)], rest[len(kinds) :]
    add_blocks(table, messages, kinds, total)
    depth = table.shape[2]
    groups = dict(zip(KINDS, group_ids()))
    rows = [table[groups[kind], 0, c] for kind in kinds for c in range(depth)]

    def renewed(i):
        return pltpu.make_async_copy(total.at[rows[i]], out.at[rows[i]], sems.at[i])

    for i, row in enumerate(rows):

        @pl.when(row >= 0)
        def _():
            renewed(i).start()

    for i, row in enumerate(rows):

        @pl.when(row >= 0)
        def _():
            renewed(i).wait()


def collect(table, messages, owned, late=4):
    depth, width, _ = messages[0].shape
    shape = (owned, width, width)
    outs = [pltpu.VMEM(shape, jnp.float32), jax.ShapeDtypeStruct(shape, jnp.float32)]
    early = len(messages) - late
    total, out = call(
        functools.partial(early_body, KINDS[:early]),
        "collect_early",
        4,
        in_specs=[SMEM] + [VMEM] * early,
        out_specs=[VMEM, ANY],
        out_shape=outs,
        scratch_shapes=[pltpu.SemaphoreType.DMA],
        cost_estimate=cost(10**9),
    )(table, *messages[:early])
    return call(
        functools.partial(late_body, KINDS[early:]),
        "collect_late",
        4,
        in_specs=[SMEM] + [VMEM] * (late + 1) + [ANY],
        out_specs=[VMEM, ANY],
        out_shape=outs,
        input_output_aliases={late + 1: 0, late + 2: 1},
        scratch_shapes=[pltpu.SemaphoreType.DMA((late * depth,))],
    )(table, *messages[early:], total, out)[1]


def per_device(
    sizes, density_blocks, send_table, batch_pairs, basis_values, previous_hartree, external_potential
):
    owned, width, _ = density_blocks.shape
    depth = send_table.shape[3]
    table = send_table.reshape(9, 1, depth)
    slots = batch_pairs.transpose(0, 2, 3, 1)
    previous = previous_hartree.transpose(1, 0, 2)
    external = external_potential.transpose(1, 0, 2)
    table_far = pltpu.with_memory_space_constraint(table, pltpu.HBM)
    blocks_far = pltpu.with_memory_space_constraint(density_blocks, pltpu.HBM)
    arrived = spread(gather(table_far, blocks_far), depth, sizes)
    turned, flat = transposed(basis_values, arrived[1], slots, len(KINDS) * depth)
    to_first, to_second, kept = density_of(flat, turned, previous, arrived, depth)
    second, first = swap(to_second, (2, 0), sizes), swap(to_first, (1, 0), sizes)
    density, sums = copied(kept, (len(KINDS) * depth + 1, width, width))
    field, charge, to_first, to_second = widen(previous, kept, first, second)
    first, second = swap(to_first, (0, 1), sizes), swap(to_second, (0, 2), sizes)
    sums = integrals_inner(flat, turned, external, field, charge, sums, sizes)
    wide = (field, charge, first, second)
    hartree, _, *partial = integrals_outer(flat, turned, external, wide, sums, depth, sizes)
    returned = [partial[0]] + [swap(m, kind, sizes) for m, kind in zip(partial[1:], KINDS[1:])]
    potential = collect(table, returned, owned)
    return density.transpose(1, 0, 2), hartree.transpose(1, 0, 2), potential


def solution(mesh):
    sizes = (mesh.shape["gx"], mesh.shape["gy"])
    in_specs = (
        P(("gx", "gy"), None, None),
        P(("gx", "gy"), None, None, None),
        P("gx", "gy", None, None),
        P("gx", "gy", None, None, None),
        P("gx", "gy", None),
        P("gx", "gy", None),
    )
    out_specs = (P("gx", "gy", None), P("gx", "gy", None), P(("gx", "gy"), None, None))
    return jax.shard_map(
        functools.partial(per_device, sizes),
        mesh=mesh,
        in_specs=in_specs,
        out_specs=out_specs,
        check_vma=False,
    )
```

```python
import functools

import jax
import jax.numpy as jnp
from jax import lax
from jax.experimental import pallas as pl
from jax.experimental.pallas import tpu as pltpu
from jax.sharding import PartitionSpec as P

SWEEPS = 3
CELL_VOLUME = 0.0625

KINDS = ((0, 0), (0, 1), (0, 2), (1, 1), (1, 2), (2, 1), (2, 2), (2, 0), (1, 0))
SENT = (((0, 0),), ((1, 0), (1, 1), (1, 2)), ((0, 1),), ((0, 2),), ((2, 1),), ((2, 2),), ((2, 0),))
ARRIVED = (((0, 0),), ((1, 0),), ((0, 1), (1, 1)), ((0, 2), (1, 2)), ((2, 1),), ((2, 2),), ((2, 0),))


def partner(index, kind):
    if kind == 0:
        return index
    return index + 1 if index % 2 == kind - 1 else index - 1


def swap(value, kind, sizes):
    count_x, count_y = sizes
    pairs = []
    for p in range(count_x):
        for q in range(count_y):
            to_p, to_q = partner(p, kind[0]), partner(q, kind[1])
            if 0 <= to_p < count_x and 0 <= to_q < count_y:
                pairs.append((p * count_y + q, to_p * count_y + to_q))
    return lax.ppermute(value, ("gx", "gy"), pairs)


def group_ids():
    p, q = lax.axis_index("gx"), lax.axis_index("gy")

    def side(index, kind):
        if kind == 0:
            return 1
        return jnp.where((index & 1) == kind - 1, 2, 0)

    return [side(p, a) * 3 + side(q, b) for a, b in KINDS]


def call(body, name, megabytes, **options):
    return pl.pallas_call(
        body,
        name=name,
        compiler_params=pltpu.CompilerParams(vmem_limit_bytes=megabytes * 1024 * 1024),
        **options,
    )


SMEM = pl.BlockSpec(memory_space=pltpu.SMEM)
VMEM = pl.BlockSpec(memory_space=pltpu.VMEM)
ANY = pl.BlockSpec(memory_space=pl.ANY)
HBM = pl.BlockSpec(memory_space=pltpu.HBM)


def gather_body(table_far, blocks_far, *rest):
    outs, (table, blocks, sems) = rest[: len(SENT)], rest[len(SENT) :]
    depth = table.shape[2]
    copies = [
        pltpu.make_async_copy(table_far, table, sems.at[0]),
        pltpu.make_async_copy(blocks_far, blocks, sems.at[1]),
    ]
    for copy in copies:
        copy.start()
    for copy in copies:
        copy.wait()
    groups = dict(zip(KINDS, group_ids()))
    for out, kinds in zip(outs, SENT):
        for part, kind in enumerate(kinds):
            for c in range(depth):
                row = jnp.maximum(table[groups[kind], 0, c], 0)
                out[part * depth + c] = blocks[row]


def gather(table, blocks):
    depth, width = table.shape[2], blocks.shape[1]
    return call(
        gather_body,
        "gather",
        12,
        in_specs=[HBM, HBM],
        out_specs=[VMEM] * len(SENT),
        out_shape=[
            jax.ShapeDtypeStruct((len(kinds) * depth, width, width), blocks.dtype)
            for kinds in SENT
        ],
        scratch_shapes=[
            pltpu.SMEM(table.shape, table.dtype),
            pltpu.VMEM(blocks.shape, blocks.dtype),
            pltpu.SemaphoreType.DMA((2,)),
        ],
    )(table, blocks)


def spread(outgoing, depth, sizes):
    own, to_first, along_first, along_second, *others = outgoing
    first = swap(to_first, (1, 0), sizes)
    two = swap(jnp.concatenate([along_second, first[2 * depth :]]), (0, 2), sizes)
    one = swap(jnp.concatenate([along_first, first[depth : 2 * depth]]), (0, 1), sizes)
    rest = [swap(blocks, kinds[0], sizes) for blocks, kinds in zip(others, SENT[4:])]
    return [own, first, one, two, *rest]


def transpose_body(empty, basis, after, slots, turned, flat, held, sems):
    brick_x, brick_y, per, _, width = basis.shape
    half = brick_y // 2
    parts = [(x, j) for x in range(brick_x) for j in range(2)]

    def coming(i):
        x, j = parts[i]
        here = pl.ds(j * half, half)
        return pltpu.make_async_copy(basis.at[x, here], held.at[x, here], sems.at[i])

    for i in range(len(parts)):
        coming(i).start()
    for i, (x, j) in enumerate(parts):
        coming(i).wait()
        for y in range(j * half, (j + 1) * half):
            for b in range(per):
                turned[x, y, b * width : (b + 1) * width, :] = held[x, y, b].T
            for pair in range(per * per):
                slot = slots[x, pair // per, pair % per, y]
                flat[(x * brick_y + y) * per * per + pair] = jnp.where(slot < 0, empty, slot)


def transposed(basis, after, slots, empty):
    brick_x, brick_y, per, points, width = basis.shape
    return call(
        functools.partial(transpose_body, empty),
        "transpose",
        32,
        in_specs=[ANY, ANY, SMEM],
        out_specs=[VMEM, SMEM],
        out_shape=[
            jax.ShapeDtypeStruct((brick_x, brick_y, per * width, points), basis.dtype),
            jax.ShapeDtypeStruct((brick_x * brick_y * per * per,), jnp.int32),
        ],
        scratch_shapes=[
            pltpu.VMEM(basis.shape, basis.dtype),
            pltpu.SemaphoreType.DMA((2 * brick_x,)),
        ],
        cost_estimate=pl.CostEstimate(flops=0, bytes_accessed=4 * basis.size, transcendentals=0),
    )(basis, after, slots)


def message_of(out, previous, density, low):
    brick_y, brick_x, _ = previous.shape
    thin = SWEEPS - 1
    out[:brick_y] = previous[...]
    per = brick_x // thin
    for y in range(brick_y):
        layers = jnp.where(low, density[y, :thin, :], density[y, brick_x - thin :, :])
        out[brick_y + y // per, (y % per) * thin : (y % per + 1) * thin, :] = layers


def density_body(depth, slots, turned, previous, *rest):
    arrived, (to_first, to_second, kept, blocks) = rest[: len(ARRIVED)], rest[len(ARRIVED) :]
    brick_x, brick_y, rows, _ = turned.shape
    width = blocks.shape[1]
    per = rows // width
    empty = len(KINDS) * depth
    groups = dict(zip(KINDS, group_ids()))
    for message, kinds in zip(arrived, ARRIVED):
        for part, kind in enumerate(kinds):
            blocks[pl.ds(groups[kind] * depth, depth)] = message[part * depth : (part + 1) * depth]
    blocks[empty] = jnp.zeros((width, width), blocks.dtype)

    def step(x, carry):
        for y in range(brick_y):
            used = [slots[(x * brick_y + y) * per * per + i] for i in range(per * per)]
            lefts = [
                jnp.concatenate([blocks[slot] for slot in used[a * per : (a + 1) * per]], axis=1)
                for a in range(per)
            ]
            right = turned[x, y]
            mixed = jnp.dot(
                jnp.concatenate(lefts, axis=0), right, preferred_element_type=jnp.float32
            )
            product = mixed * right.astype(jnp.float32)
            kept[y, pl.ds(x, 1), :] = jnp.sum(product, axis=0, keepdims=True)
        return carry

    lax.fori_loop(0, brick_x, step, 0)
    odd = (lax.axis_index("gx") & 1) == 1
    message_of(to_first, previous, kept, odd)
    message_of(to_second, previous, kept, jnp.logical_not(odd))


def density_of(slots, turned, previous, arrived, depth):
    brick_x, brick_y, rows, points = turned.shape
    width = arrived[0].shape[1]
    thin = SWEEPS - 1
    shape = (brick_y, brick_x, points)
    message = jax.ShapeDtypeStruct((brick_y + brick_y * thin // brick_x, brick_x, points), jnp.float32)
    return call(
        functools.partial(density_body, depth),
        "density",
        12,
        in_specs=[SMEM] + [VMEM] * (2 + len(arrived)),
        out_specs=[VMEM] * 3,
        out_shape=[message, message, jax.ShapeDtypeStruct(shape, jnp.float32)],
        scratch_shapes=[pltpu.VMEM((len(KINDS) * depth + 1, width, width), turned.dtype)],
    )(slots, turned, previous, *arrived)


def copied_body(kept, density, sums):
    density[...] = kept[...]
    sums[...] = jnp.zeros_like(sums)


def copied(kept, shape):
    return call(
        copied_body,
        "copied",
        4,
        in_specs=[VMEM],
        out_specs=[VMEM] * 2,
        out_shape=[jax.ShapeDtypeStruct(kept.shape, kept.dtype), pltpu.VMEM(shape, jnp.float32)],
    )(kept)


def cost(flops):
    return pl.CostEstimate(flops=flops, bytes_accessed=0, transcendentals=0)


def sides(axis, first, second):
    even = (lax.axis_index(axis) & 1) == 0
    return jnp.where(even, second, first), jnp.where(even, first, second)


def widen_body(previous, density, first, second, field, charge, to_first, to_second):
    wide, thin = SWEEPS, SWEEPS - 1
    brick_y, brick_x, points = density.shape
    per = brick_x // thin
    before, after = sides("gx", first[...], second[...])
    field[...] = jnp.zeros_like(field)
    field[:, :wide, :] = before[:brick_y, brick_x - wide :, :]
    field[:, wide : wide + brick_x, :] = previous[...]
    field[:, wide + brick_x : 2 * wide + brick_x, :] = after[:brick_y, :wide, :]
    charge[:, thin : thin + brick_x, :] = density[...]
    for y in range(brick_y):
        row, start = brick_y + y // per, (y % per) * thin
        charge[y, :thin, :] = before[row, start : start + thin, :]
        charge[y, thin + brick_x :, :] = after[row, start : start + thin, :]
    width = brick_x + 2 * thin
    even = (lax.axis_index("gy") & 1) == 0
    low = [field[:wide, 1 : 1 + width, :], charge[:thin]]
    high = [field[brick_y - wide :, 1 : 1 + width, :], charge[brick_y - thin :]]
    for out, where_even, where_odd in ((to_first, high, low), (to_second, low, high)):
        out[:wide] = jnp.where(even, where_even[0], where_odd[0])
        out[wide:] = jnp.where(even, where_even[1], where_odd[1])


def widen(previous, density, first, second):
    brick_y, brick_x, points = density.shape
    wide, thin = SWEEPS, SWEEPS - 1
    width = brick_x + 2 * thin
    shapes = [(brick_y, 16, points), (brick_y, width, points)] + [(wide + thin, width, points)] * 2
    return call(
        widen_body,
        "widen",
        4,
        in_specs=[VMEM] * 4,
        out_specs=[VMEM] * 4,
        out_shape=[jax.ShapeDtypeStruct(shape, jnp.float32) for shape in shapes],
    )(previous, density, first, second)


def sweeps_in(field, field_y, charge, charge_y, first, last, brick_y, sizes, steps):
    points = field.shape[2]
    brick_x = charge.shape[1] - 2 * (SWEEPS - 1)
    p, q = lax.axis_index("gx"), lax.axis_index("gy")
    source, source_y = field, field_y
    for done in range(1, SWEEPS + 1):
        margin = SWEEPS - done
        start, stop = first - margin, last + margin
        rows, columns = stop - start, brick_x + 2 * margin
        row, skip = start - source_y, SWEEPS - 1 - margin
        here = source[row : row + rows, 1 : 1 + columns, :]
        z = lax.broadcasted_iota(jnp.int32, here.shape, 2)
        total = source[row - 1 : row - 1 + rows, 1 : 1 + columns, :]
        total += source[row + 1 : row + 1 + rows, 1 : 1 + columns, :]
        total += source[row : row + rows, :columns, :]
        total += source[row : row + rows, 2 : 2 + columns, :]
        total += jnp.where(z == 0, 0.0, pltpu.roll(here, 1, 2))
        total += jnp.where(z == points - 1, 0.0, pltpu.roll(here, points - 1, 2))
        row = start - charge_y
        value = (total + charge[row : row + rows, skip : skip + columns, :]) * (1.0 / 6.0)
        if margin == 0:
            return value
        source, source_y = steps[done - 1], start
        source[:rows, :columns, :] = value

        def clear(condition, rows_out, columns_out):
            @pl.when(condition)
            def _():
                part = source[rows_out, columns_out, :]
                source[rows_out, columns_out, :] = jnp.zeros_like(part)

        clear(p == 0, slice(0, rows), slice(0, margin))
        clear(p == sizes[0] - 1, slice(0, rows), slice(margin + brick_x, columns))
        if start < 0:
            clear(q == 0, slice(0, -start), slice(0, columns))
        if stop > brick_y:
            clear(q == sizes[1] - 1, slice(brick_y - start, rows), slice(0, columns))


def lengthen(field_x, charge_x, first, second, field, charge):
    wide, thin = SWEEPS, SWEEPS - 1
    brick_y, width, _ = charge_x.shape
    before, after = sides("gy", first[...], second[...])
    field[:wide, 1 : 1 + width, :] = before[:wide]
    field[wide : wide + brick_y] = field_x[...]
    field[wide + brick_y :, 1 : 1 + width, :] = after[:wide]
    charge[:thin] = before[wide:]
    charge[thin : thin + brick_y] = charge_x[...]
    charge[thin + brick_y :] = after[wide:]


def add_integrals(slots, turned, potential, sums, columns):
    width = sums.shape[1]
    per = turned.shape[2] // width
    brick_y = turned.shape[1]

    def step(i, carry):
        for x, y in [(2 * i + j, y) for j in range(2) for y in columns]:
            left = turned[x, y]
            weighted = left.astype(jnp.float32) * potential[y, pl.ds(x, 1), :]
            product = lax.dot_general(
                left,
                weighted.astype(turned.dtype),
                (((1,), (1,)), ((), ())),
                preferred_element_type=jnp.float32,
            )
            for a in range(per):
                for b in range(per):
                    slot = slots[(x * brick_y + y) * per * per + a * per + b]
                    sums[slot] += product[a * width : (a + 1) * width, b * width : (b + 1) * width]
        return carry

    lax.fori_loop(0, turned.shape[0] // 2, step, 0)


def inner_body(sizes, slots, turned, external, field_x, charge_x, _, sums, potential, *steps):
    brick_y = external.shape[0]
    first, last = SWEEPS, brick_y - SWEEPS
    swept = sweeps_in(field_x, 0, charge_x, 0, first, last, brick_y, sizes, steps)
    potential[first:last] = swept + external[first:last]
    add_integrals(slots, turned, potential, sums, range(first, last))


def outer_body(depth, sizes, slots, turned, external, *rest):
    kinds = len(KINDS)
    wide, rest = rest[:4], rest[5:]
    hartree, sums, outs = rest[0], rest[1], rest[2 : 2 + kinds]
    potential, *steps = rest[2 + kinds : 2 + kinds + SWEEPS]
    field, charge, swept, sem = rest[2 + kinds + SWEEPS :]
    brick_y = external.shape[0]
    field[...] = jnp.zeros_like(field)
    lengthen(*wide, field, charge)
    swept[...] = sweeps_in(field, -SWEEPS, charge, 1 - SWEEPS, 0, brick_y, brick_y, sizes, steps)
    copy = pltpu.make_async_copy(swept, hartree, sem)
    copy.start()
    potential[...] = swept[...] + external[...]
    columns = [*range(SWEEPS), *range(brick_y - SWEEPS, brick_y)]
    add_integrals(slots, turned, potential, sums, columns)
    for group, out in zip(group_ids(), outs):
        part = sums[pl.ds(group * depth, depth)]
        out[...] = (CELL_VOLUME * part).astype(out.dtype)
    copy.wait()


def sweep_scratch(brick_y, brick_x, points):
    return [pltpu.VMEM((brick_y, brick_x, points), jnp.float32)] + [
        pltpu.VMEM((brick_y + 2 * margin, 8, points), jnp.float32)
        for margin in range(SWEEPS - 1, 0, -1)
    ]


def integrals_inner(slots, turned, external, field, charge, sums, sizes):
    return call(
        functools.partial(inner_body, sizes),
        "integrals_inner",
        8,
        in_specs=[SMEM] + [VMEM] * 5,
        out_specs=VMEM,
        out_shape=pltpu.VMEM(sums.shape, sums.dtype),
        input_output_aliases={5: 0},
        scratch_shapes=sweep_scratch(*external.shape),
        cost_estimate=cost(turned.size * turned.shape[2]),
    )(slots, turned, external, field, charge, sums)


def integrals_outer(slots, turned, external, wide, sums, depth, sizes):
    kinds = len(KINDS)
    shape = (depth,) + sums.shape[1:]
    brick_y, brick_x, points = external.shape
    return call(
        functools.partial(outer_body, depth, sizes),
        "integrals_outer",
        12,
        in_specs=[SMEM] + [VMEM] * 7,
        out_specs=[ANY] + [VMEM] * (1 + kinds),
        out_shape=[
            jax.ShapeDtypeStruct(external.shape, jnp.float32),
            pltpu.VMEM(sums.shape, sums.dtype),
            jax.ShapeDtypeStruct(shape, jnp.float32),
        ]
        + [jax.ShapeDtypeStruct(shape, jnp.bfloat16)] * (kinds - 1),
        input_output_aliases={7: 1},
        scratch_shapes=sweep_scratch(*external.shape)
        + [
            pltpu.VMEM((brick_y + 2 * SWEEPS, 16, points), jnp.float32),
            pltpu.VMEM((brick_y + 2 * SWEEPS - 2, brick_x + 2 * SWEEPS - 2, points), jnp.float32),
            pltpu.VMEM(external.shape, jnp.float32),
            pltpu.SemaphoreType.DMA,
        ],
        cost_estimate=cost(turned.size * turned.shape[2]),
    )(slots, turned, external, *wide, sums)


def add_blocks(table, messages, kinds, out):
    depth = table.shape[2]
    groups = dict(zip(KINDS, group_ids()))
    for message, kind in zip(messages, kinds):
        for c in range(depth):
            row = table[groups[kind], 0, c]

            @pl.when(row >= 0)
            def _():
                out[row] += message[c].astype(jnp.float32)


def early_body(kinds, table, *rest):
    messages, (total, out, sem) = rest[: len(kinds)], rest[len(kinds) :]
    total[...] = jnp.zeros_like(total)
    add_blocks(table, messages, kinds, total)
    copy = pltpu.make_async_copy(total, out, sem)
    copy.start()
    copy.wait()


def late_body(kinds, table, *rest):
    messages, (_, _, total, out, sems) = rest[: len(kinds)], rest[len(kinds) :]
    add_blocks(table, messages, kinds, total)
    depth = table.shape[2]
    groups = dict(zip(KINDS, group_ids()))
    rows = [table[groups[kind], 0, c] for kind in kinds for c in range(depth)]

    def renewed(i):
        return pltpu.make_async_copy(total.at[rows[i]], out.at[rows[i]], sems.at[i])

    for i, row in enumerate(rows):

        @pl.when(row >= 0)
        def _():
            renewed(i).start()

    for i, row in enumerate(rows):

        @pl.when(row >= 0)
        def _():
            renewed(i).wait()


def collect(table, messages, owned, late=4):
    depth, width, _ = messages[0].shape
    shape = (owned, width, width)
    outs = [pltpu.VMEM(shape, jnp.float32), jax.ShapeDtypeStruct(shape, jnp.float32)]
    early = len(messages) - late
    total, out = call(
        functools.partial(early_body, KINDS[:early]),
        "collect_early",
        4,
        in_specs=[SMEM] + [VMEM] * early,
        out_specs=[VMEM, ANY],
        out_shape=outs,
        scratch_shapes=[pltpu.SemaphoreType.DMA],
        cost_estimate=cost(10**9),
    )(table, *messages[:early])
    return call(
        functools.partial(late_body, KINDS[early:]),
        "collect_late",
        4,
        in_specs=[SMEM] + [VMEM] * (late + 1) + [ANY],
        out_specs=[VMEM, ANY],
        out_shape=outs,
        input_output_aliases={late + 1: 0, late + 2: 1},
        scratch_shapes=[pltpu.SemaphoreType.DMA((late * depth,))],
    )(table, *messages[early:], total, out)[1]


def per_device(
    sizes, density_blocks, send_table, batch_pairs, basis_values, previous_hartree, external_potential
):
    owned, width, _ = density_blocks.shape
    depth = send_table.shape[3]
    table = send_table.reshape(9, 1, depth)
    slots = batch_pairs.transpose(0, 2, 3, 1)
    previous = previous_hartree.transpose(1, 0, 2)
    external = external_potential.transpose(1, 0, 2)
    table_far = pltpu.with_memory_space_constraint(table, pltpu.HBM)
    blocks_far = pltpu.with_memory_space_constraint(density_blocks, pltpu.HBM)
    arrived = spread(gather(table_far, blocks_far), depth, sizes)
    turned, flat = transposed(basis_values, arrived[1], slots, len(KINDS) * depth)
    to_first, to_second, kept = density_of(flat, turned, previous, arrived, depth)
    second, first = swap(to_second, (2, 0), sizes), swap(to_first, (1, 0), sizes)
    density, sums = copied(kept, (len(KINDS) * depth + 1, width, width))
    field, charge, to_first, to_second = widen(previous, kept, first, second)
    first, second = swap(to_first, (0, 1), sizes), swap(to_second, (0, 2), sizes)
    sums = integrals_inner(flat, turned, external, field, charge, sums, sizes)
    wide = (field, charge, first, second)
    hartree, _, *partial = integrals_outer(flat, turned, external, wide, sums, depth, sizes)
    returned = [partial[0]] + [swap(m, kind, sizes) for m, kind in zip(partial[1:], KINDS[1:])]
    potential = collect(table, returned, owned)
    return density.transpose(1, 0, 2), hartree.transpose(1, 0, 2), potential


def solution(mesh):
    sizes = (mesh.shape["gx"], mesh.shape["gy"])
    in_specs = (
        P(("gx", "gy"), None, None),
        P(("gx", "gy"), None, None, None),
        P("gx", "gy", None, None),
        P("gx", "gy", None, None, None),
        P("gx", "gy", None),
        P("gx", "gy", None),
    )
    out_specs = (P("gx", "gy", None), P("gx", "gy", None), P(("gx", "gy"), None, None))
    return jax.shard_map(
        functools.partial(per_device, sizes),
        mesh=mesh,
        in_specs=in_specs,
        out_specs=out_specs,
        check_vma=False,
    )
```
